32 devices in a mesh: rows: 16 (over z, x, core), heads: 2 (over y).
Axes of the slice: x: 2, y: 2, z: 4, core: 2. Of those that a mesh axis runs over, the one named last changes fastest.
Arguments:
- inputs: bfloat16 [8192, 2048], P('rows'), may hold values from -6 to 6
- memory_keep: int32 [8192], P('rows'), may hold values from 0 to 1, as said below
- feature_present: int32 [8192, 64], P('rows'), may hold values 0 or 1
- w_query: bfloat16 [2048, 256], P(None, 'heads'), may hold values from -0.125 to 0.125
- w_key: bfloat16 [2048, 256], P(None, 'heads'), may hold values from -0.125 to 0.125
- w_value: bfloat16 [2048, 256], P(None, 'heads'), may hold values from -0.125 to 0.125
- beta_sample: float32 [8], P('heads'), may hold values from 0.18 to 0.45
- w_out: bfloat16 [256, 2048], replicated, may hold values from -3.5 to 3.5
- norm_gain: float32 [2048], replicated, may hold values from 0.5 to 1.5
- norm_bias: float32 [2048], replicated, may hold values from -1.75 to 1.75
- wf_query: bfloat16 [32, 256], replicated, may hold values from -1 to 1
- wf_key: bfloat16 [32, 256], replicated, may hold values from -1 to 1
- wf_value: bfloat16 [32, 256], replicated, may hold values from -1 to 1
- beta_feature: float32 [8], replicated, may hold values from 0.18 to 0.45
- wf_out: bfloat16 [256, 32], replicated, may hold values from -1 to 1
- cotangent: bfloat16 [8192, 2048], P('rows', 'heads'), may hold values from -6 to 6
Outputs:
- block_out: bfloat16 [8192, 2048], P('rows', 'heads')
- input_grad: bfloat16 [8192, 2048], P('rows')
- grad_query: float32 [2048, 256], P(None, 'heads')
- grad_key: float32 [2048, 256], P(None, 'heads')
- grad_value: float32 [2048, 256], P(None, 'heads')
- grad_beta_sample: float32 [8], P('heads')
- grad_out: float32 [256, 2048], replicated
- grad_gain: float32 [2048], replicated
- grad_bias: float32 [2048], replicated
- grad_fquery: float32 [32, 256], replicated
- grad_fkey: float32 [32, 256], replicated
- grad_fvalue: float32 [32, 256], replicated
- grad_beta_feature: float32 [8], replicated
- grad_fout: float32 [256, 32], replicated
The draws below stay inside these ranges and needn't reach their ends.
Inputs may be any that keep to these rules, and one draw needn't show every extreme that they name: `memory_keep`: each entry is 0 or 1, and at least two of the 8192 rows hold 1.
All inputs are finite; a program needn't handle non-finite values. No bound on the sum of `feature_present` on one device may be relied on, other than what follows from the above.
Results may differ from the reference program's by a relative error of at most 0.04.
Values may be sent and summed in bfloat16 or wider, within the bound.
No kernel may reach another device: no remote copies, remote signals or barrier semaphores. Data moves between devices by JAX's collectives and lax.ppermute only.
A program may use at most 448 MiB of HBM per device.

```python
import math
import jax
import jax.numpy as jnp
from jax import lax

F = 64
E = 32
H = 8
HD = 32
N = 8192
S = 2048
A = 256


def draw_memory_keep(key, part):
    key = jax.random.fold_in(key, 7)
    first_key, second_key = jax.random.split(key)
    levels = jax.random.randint(first_key, (N,), 0, 4)
    keep_rows = jnp.where(levels > 0, 1, 0).astype(jnp.int32)
    chosen = jax.random.permutation(second_key, N)[:2]
    return keep_rows.at[chosen].set(1)


def set_ends(array, stream_key, least, top_value):
    longest = array.shape.index(max(array.shape))
    spots = []
    for shift in (0, 1):
        where = [jax.random.randint(jax.random.fold_in(stream_key, axis), (), 0, length) for axis, length in enumerate(array.shape)]
        where[longest] = (where[longest] + shift) % array.shape[longest]
        spots.append(tuple(where))
    return array.at[spots[0]].set(least).at[spots[1]].set(top_value)


def block_levels(key, extent, cuts, smallest, high):
    def one(dim, shards_of):
        draws = jax.random.uniform(jax.random.fold_in(jax.random.fold_in(key, 6), dim), (shards_of,), jnp.float32, smallest / len(cuts), high / len(cuts))
        return jnp.repeat(jnp.exp(draws), extent[dim] // shards_of).reshape((-1,) + (1,) * (len(extent) - dim - 1))

    factor_of = one(*cuts[0])
    for cut in cuts[1:]:
        factor_of = factor_of * one(*cut)
    return factor_of


def noise(own_key, shape, spread, bound, pieces=(), kind=jnp.bfloat16):
    drawn = spread * jax.random.normal(own_key, shape, jnp.float32)
    if pieces:
        drawn = drawn * block_levels(own_key, shape, pieces, -0.22, 0.18)
    return jnp.clip(drawn, -bound, bound).astype(kind)


def setup_inputs(seed: int = 0) -> dict:
    seeds = jax.random.split(jax.random.key(seed), 17)
    return {
        "inputs": noise(seeds[0], (N, S), 1.0, 6.0, ((0, 16),)),
        "memory_keep": draw_memory_keep(jax.random.fold_in(seeds[16], 71), 0),
        "feature_present": set_ends((jax.random.randint(seeds[2], (N, F), 0, 8) < 7).astype(jnp.int32), jax.random.fold_in(seeds[2], 1), 0, 1),
        "w_query": noise(seeds[3], (S, A), S ** -0.5, 0.125, ((1, 2),)),
        "w_key": noise(seeds[4], (S, A), S ** -0.5, 0.125, ((1, 2),)),
        "w_value": noise(seeds[5], (S, A), S ** -0.5, 0.125, ((1, 2),)),
        "beta_sample": jnp.clip(jnp.exp(math.log(0.45) - 0.91629067 * jax.random.uniform(seeds[6], (H,), jnp.float32) ** block_levels(seeds[6], (H,), ((0, 2),), -0.2, 0.2)), 0.18, 0.45),
        "w_out": noise(seeds[7], (A, S), (0.006 * N ** 0.5), 3.5),
        "norm_gain": jnp.clip(1.0 + 0.1 * jax.random.normal(seeds[8], (S,), jnp.float32), 0.5, 1.5),
        "norm_bias": noise(seeds[9], (S,), 0.3, 1.75, (), jnp.float32),
        "wf_query": noise(seeds[10], (E, A), E ** -0.5, 1.0),
        "wf_key": noise(seeds[11], (E, A), E ** -0.5, 1.0),
        "wf_value": noise(seeds[12], (E, A), E ** -0.5, 1.0),
        "beta_feature": jnp.clip(jnp.exp(jax.random.uniform(seeds[13], (H,), jnp.float32, math.log(0.18), math.log(0.45))), 0.18, 0.45),
        "wf_out": noise(seeds[14], (A, E), (A // 8) ** -0.5, 1.0),
        "cotangent": noise(seeds[15], (N, S), 1.0, 6.0, ((0, 16), (1, 2))),
    }


NEG_FILL = -1e+30
NORM_EPS = 1e-05
HIGHEST = lax.Precision.HIGHEST

@jax.custom_vjp
def low(v):
    return lax.optimization_barrier(v.astype(jnp.bfloat16)).astype(jnp.float32)

@jax.custom_vjp
def low_back(v):
    return v

def low_keep(v):
    return (low(v), None)

def low_pass(kept, grad):
    return (grad,)

def back_keep(v):
    return (v, None)

def back_low(kept, grad):
    return (low(grad),)
low.defvjp(low_keep, low_pass)
low_back.defvjp(back_keep, back_low)

def sample_attention(queries, key_rows, value_rows, memory_keep, beta_sample):
    total_rows = queries.shape[0]
    block_rows = math.gcd(total_rows, 512)
    blocks = total_rows // block_rows
    key_index = jnp.arange(total_rows, dtype=jnp.int32)
    firsts = jnp.arange(blocks, dtype=jnp.int32) * block_rows

    def one_block(block_data):
        query_block, first_row = block_data
        query_index = first_row + jnp.arange(block_rows, dtype=jnp.int32)
        raw_scores = low_back(jnp.einsum('qhd,khd->hqk', query_block, key_rows, precision=HIGHEST))
        allowed = (memory_keep[None, None, :] > 0) & (query_index[None, :, None] != key_index[None, None, :])
        scores = jnp.where(allowed, beta_sample[:, None, None] * raw_scores, NEG_FILL)
        row_max = lax.optimization_barrier(jnp.max(scores, axis=-1, keepdims=True))
        exp_terms = jnp.where(allowed, jnp.exp(scores - row_max), 0.0)
        prob_low = low(exp_terms / lax.optimization_barrier(jnp.sum(exp_terms, axis=-1, keepdims=True)))
        return jnp.einsum('hqk,khd->qhd', prob_low, value_rows, precision=HIGHEST)
    result = lax.map(jax.checkpoint(one_block), (queries.reshape(blocks, block_rows, H, HD), firsts))
    return result.reshape(total_rows, H * HD)

def feature_attention(feat_query, feat_key, feat_value, feature_present, beta_feature):
    total_rows = feat_query.shape[0]
    block_rows = math.gcd(total_rows, 512)
    blocks = total_rows // block_rows
    diagonal = jnp.eye(F, dtype=bool)

    def one_block(block_data):
        query_block, key_block, value_block, present_block = block_data
        raw_scores = jnp.einsum('nqhd,nkhd->nhqk', query_block, key_block, precision=HIGHEST)
        allowed = (present_block[:, None, None, :] > 0) | diagonal[None, None, :, :]
        scores = jnp.where(allowed, beta_feature[None, :, None, None] * raw_scores, NEG_FILL)
        row_max = lax.optimization_barrier(jnp.max(scores, axis=-1, keepdims=True))
        exp_terms = jnp.where(allowed, jnp.exp(scores - row_max), 0.0)
        prob_low = low(exp_terms / lax.optimization_barrier(jnp.sum(exp_terms, axis=-1, keepdims=True)))
        return jnp.einsum('nhqk,nkhd->nqhd', prob_low, value_block, precision=HIGHEST)
    stacked = (feat_query.reshape(blocks, block_rows, F, H, HD), feat_key.reshape(blocks, block_rows, F, H, HD), feat_value.reshape(blocks, block_rows, F, H, HD), feature_present.reshape(blocks, block_rows, F))
    result = lax.map(jax.checkpoint(one_block), stacked)
    return result.reshape(total_rows, F, H * HD)

def reference(inputs, memory_keep, feature_present, w_query, w_key, w_value, beta_sample, w_out, norm_gain, norm_bias, wf_query, wf_key, wf_value, beta_feature, wf_out, cotangent):

    def forward(inputs_f, weight_query, weight_key, weight_value, beta_heads, weight_out, gain_row, bias_row, weight_fquery, weight_fkey, weight_fvalue, beta_tokens, weight_fout):
        total_rows = inputs_f.shape[0]
        queries = low_back(low(jnp.dot(inputs_f, weight_query, precision=HIGHEST))).reshape(total_rows, H, HD)
        key_rows = low_back(low(jnp.dot(inputs_f, weight_key, precision=HIGHEST))).reshape(total_rows, H, HD)
        value_rows = low_back(low(jnp.dot(inputs_f, weight_value, precision=HIGHEST))).reshape(total_rows, H, HD)
        retrieved = low_back(low(sample_attention(queries, key_rows, value_rows, memory_keep, beta_heads)))
        hidden = inputs_f + low_back(jnp.dot(retrieved, weight_out, precision=HIGHEST))
        centred = hidden - lax.optimization_barrier(jnp.mean(hidden, axis=-1, keepdims=True))
        variance = lax.optimization_barrier(jnp.mean(centred * centred, axis=-1, keepdims=True))
        unit_rows = centred * lax.rsqrt(variance + NORM_EPS) * gain_row + bias_row
        tokens = low(unit_rows).reshape(total_rows, F, E)
        feat_query = low_back(low(jnp.einsum('nfe,ea->nfa', tokens, weight_fquery, precision=HIGHEST)))
        feat_key = low_back(low(jnp.einsum('nfe,ea->nfa', tokens, weight_fkey, precision=HIGHEST)))
        feat_value = low_back(low(jnp.einsum('nfe,ea->nfa', tokens, weight_fvalue, precision=HIGHEST)))
        feat_out = low_back(low(feature_attention(feat_query, feat_key, feat_value, feature_present, beta_tokens)))
        change_rows = jnp.einsum('nfa,ae->nfe', feat_out, weight_fout, precision=HIGHEST).reshape(total_rows, F * E)
        return unit_rows + change_rows
    block_out, pullback = jax.vjp(forward, inputs.astype(jnp.float32), w_query.astype(jnp.float32), w_key.astype(jnp.float32), w_value.astype(jnp.float32), beta_sample, w_out.astype(jnp.float32), norm_gain, norm_bias, wf_query.astype(jnp.float32), wf_key.astype(jnp.float32), wf_value.astype(jnp.float32), beta_feature, wf_out.astype(jnp.float32))
    gradients = pullback(cotangent.astype(jnp.float32))
    return (block_out.astype(jnp.bfloat16), gradients[0].astype(jnp.bfloat16), gradients[1], gradients[2], gradients[3], gradients[4], gradients[5], gradients[6], gradients[7], gradients[8], gradients[9], gradients[10], gradients[11], gradients[12])
```

```python
from functools import partial

import jax
import jax.numpy as jnp
from jax import lax
from jax.experimental import pallas as pl
from jax.experimental.pallas import tpu as pltpu
from jax.sharding import Mesh, PartitionSpec as P

BF = jnp.bfloat16
F32 = jnp.float32
NEG = -1e30
FLAG = 1e30
NORM_EPS = 1e-05
LOG2E = 1.4426950408889634
SUM_LIMIT = 2.0**60
VMEM_BYTES = 56 * 1024 * 1024
GROUP = 8
STEP_GROUPS = 4
EDGE_GROUPS = 8


def dot(a, b):
    return jnp.dot(a, b, preferred_element_type=F32)


def dot_last(a, b):
    return lax.dot_general(a, b, (((1,), (1,)), ((), ())), preferred_element_type=F32)


def split_dot(a, b_ref, pieces):
    depth = a.shape[1] // pieces
    terms = [
        dot(a[:, j * depth : (j + 1) * depth], b_ref[j * depth : (j + 1) * depth, :])
        for j in range(pieces)
    ]
    while len(terms) > 1:
        terms = [x + y for x, y in zip(terms[::2], terms[1::2])]
    return terms[0]


def params(steps=0):
    return pltpu.CompilerParams(
        vmem_limit_bytes=VMEM_BYTES,
        dimension_semantics=("arbitrary",) * steps if steps else None,
    )


def three_parts(x):
    high = x.astype(BF)
    rest = x - high.astype(F32)
    mid = rest.astype(BF)
    low = (rest - mid.astype(F32)).astype(BF)
    return high, mid, low


def project_kernel(lane_ref, x_ref, wq_ref, wk_ref, wv_ref, keep_ref, *rest):
    *outs, joined_ref, turned_ref, sem = rest
    copies = [
        pltpu.make_async_copy(w_ref, joined_ref.at[place], sem.at[place])
        for place, w_ref in enumerate((wq_ref, wk_ref, wv_ref))
    ]

    @pl.when(pl.program_id(0) == 0)
    def _():
        for copy in copies:
            copy.start()

    rows3, _ = outs[0].shape
    size = rows3 // 3
    x = x_ref[...]
    for place, w_ref in enumerate((wq_ref, wk_ref, wv_ref)):
        turned = split_dot(x, w_ref, 4).T
        if place == 1:
            turned = jnp.where(keep_ref[...] > 0, turned, FLAG)
        turned_ref[...] = turned
        for relative, out_ref in enumerate(outs):
            head = pl.multiple_of((lane_ref[0] ^ relative) * size, size)
            out_ref[place * size : (place + 1) * size, :] = turned_ref[pl.ds(head, size), :].astype(
                BF
            )

    @pl.when(pl.program_id(0) == pl.num_programs(0) - 1)
    def _():
        for copy in copies:
            copy.wait()


def project(lane, inputs, w_query, w_key, w_value, keep, heads):
    rows, width = inputs.shape
    local = w_query.shape[1]
    size = local // heads
    block = min(rows, 256)
    weight = pl.BlockSpec(memory_space=pltpu.VMEM)
    return pl.pallas_call(
        project_kernel,
        grid=(rows // block,),
        in_specs=[
            pl.BlockSpec(memory_space=pltpu.SMEM),
            pl.BlockSpec((block, width), lambda i: (i, 0)),
            weight,
            weight,
            weight,
            pl.BlockSpec((1, block), lambda i: (0, i)),
        ],
        out_specs=[pl.BlockSpec((3 * size, block), lambda i: (0, i))] * heads
        + [pl.BlockSpec(memory_space=pl.ANY)],
        out_shape=[jax.ShapeDtypeStruct((3 * size, rows), BF)] * heads
        + [jax.ShapeDtypeStruct((3, width, local), BF)],
        scratch_shapes=[pltpu.VMEM((local, block), F32), pltpu.SemaphoreType.DMA((3,))],
        compiler_params=params(1),
        cost_estimate=pl.CostEstimate(
            flops=6 * rows * width * local,
            bytes_accessed=2 * (rows * width + 3 * width * local),
            transcendentals=0,
        ),
        name="project",
    )(lane.reshape(1), inputs, w_query, w_key, w_value, keep.reshape(1, rows))


def lay_rows(ref, first, last):
    return jnp.concatenate([ref[s, first:last, :] for s in range(ref.shape[0])], axis=1)


def build_keys(kv_ref, kaug_ref, size):
    keys = lay_rows(kv_ref, 0, size).astype(F32)
    flagged = keys[0:1, :] > 0.5 * FLAG
    clean = jnp.where(flagged, 0.0, keys)
    count = keys.shape[1]
    row = lax.broadcasted_iota(jnp.int32, (size, count), 0)
    bias = jnp.where(flagged, NEG, 0.0)
    extra = jnp.where(row == 0, bias, jnp.where(row < 4, 1.0, 0.0))
    clean = clean.astype(BF)
    kaug_ref[...] = jnp.concatenate([clean, clean, clean, extra.astype(BF)], axis=0).T


def build_queries(beta, q_ref, qaug_ref, size):
    queries = lay_rows(q_ref, 0, size).astype(F32) * (beta * LOG2E)
    row = lax.broadcasted_iota(jnp.int32, queries.shape, 0)
    high, mid, low = three_parts(queries)
    qaug_ref[0:size, :] = high
    qaug_ref[size : 2 * size, :] = mid
    qaug_ref[2 * size : 3 * size, :] = low
    qaug_ref[3 * size : 4 * size, :] = jnp.where(row == 0, 1.0, 0.0).astype(BF)


def hide_own(scores, first_key, first_query):
    key = lax.broadcasted_iota(jnp.int32, scores.shape, 0) + first_key
    query = lax.broadcasted_iota(jnp.int32, scores.shape, 1) + first_query
    return jnp.where(key == query, NEG, scores)


def forward_kernel(lane_ref, beta_ref, q_ref, kv_ref, *rest, own, last, size, span):
    if own:
        carry_ref = None
    else:
        carry_ref, rest = rest[0], rest[1:]
    far_ref, *outs = rest[:-5]
    qaug_ref, kaug_ref, vaug_ref, kept_ref, sem = rest[-5:]
    step = pl.program_id(0)
    keys, block = kept_ref.shape[1:]

    @pl.when(step == 0)
    def _():
        build_keys(kv_ref, kaug_ref, size)
        build_queries(beta_ref[0], q_ref, qaug_ref, size)
        vaug_ref[0:size, :] = lay_rows(kv_ref, size, 2 * size)
        row = lax.broadcasted_iota(jnp.int32, (16, keys), 0)
        vaug_ref[size : size + 16, :] = jnp.where(row == 0, 1.0, 0.0).astype(BF)

    cols = pl.ds(pl.multiple_of(step * block, block), block)
    extra_rows = lax.broadcasted_iota(jnp.int32, (16, block), 0)

    def scores_of(j):
        scores = dot(kaug_ref[j * span : (j + 1) * span, :], qaug_ref[:, cols])
        if own:
            scores = hide_own(scores, j * span, step * block)
        return scores

    def set_shift(shift):
        extra = jnp.where(extra_rows == 0, 1.0, 0.0)
        for row, part in enumerate(three_parts(-shift)):
            extra = jnp.where(extra_rows == row + 1, part.astype(F32), extra)
        qaug_ref[3 * size : 3 * size + 16, cols] = extra.astype(BF)

    def set_maximum(least):
        tops = jnp.full((8, block), 2 * NEG, F32)
        for j in range(keys // span):
            tops = jnp.maximum(tops, jnp.max(scores_of(j).reshape(span // 8, 8, block), axis=0))
        top = jnp.max(tops, axis=0, keepdims=True)
        if least is not None:
            top = jnp.maximum(top, least)
        set_shift(top)
        return top

    def copy_out(at, j):
        rows = slice(j * span, (j + 1) * span)
        lanes = pl.ds(pl.multiple_of(at * block, block), block)
        return pltpu.make_async_copy(
            kept_ref.at[at, rows, :], far_ref.at[rows, lanes], sem.at[at, j]
        )

    def weigh():
        count = keys // span
        half = count // 2
        ahead = scores_of(0)
        total = None
        for j in range(count):
            scores = ahead
            if j + 1 < count:
                ahead = scores_of(j + 1)
            if j == half + 2:
                total = dot(vaug_ref[:, : half * span], kept_ref[step, : half * span, :])
            kept_ref[step, j * span : (j + 1) * span, :] = jnp.exp2(scores).astype(BF)
            copy_out(step, j).start()
        return total + dot(vaug_ref[:, half * span :], kept_ref[step, half * span :, :])

    stat_ref = outs[-1]

    def finish(total, top):
        if last:
            ret_ref = outs[0]
            summed = total[size : size + 1, :]
            result = total[0:size, :] / summed
            places, _, piece = ret_ref.shape
            parts = places // q_ref.shape[0]
            for j in range(block // piece):
                lane = (step * (block // piece // parts) + j // parts) ^ lane_ref[0]
                ret_ref[lane * parts + j % parts] = result[:, j * piece : (j + 1) * piece].astype(BF)
            stat_ref[0:size, cols] = result
            stat_ref[size : size + 8, cols] = jnp.broadcast_to(top + jnp.log2(summed), (8, block))
        else:
            stat_ref[0:40, cols] = total[0:40, :]
        stat_ref[40:48, cols] = jnp.broadcast_to(top, (8, block))

    old = None if own else carry_ref[40:41, cols]
    if not own:
        set_shift(old)
    total = weigh()
    sums = total[size : size + 1, :]
    fits = jnp.max(sums) < SUM_LIMIT
    if own:
        fits = jnp.logical_and(fits, jnp.min(sums) > 1.0 / SUM_LIMIT)
        finish(total, jnp.zeros((1, block), F32))
    else:
        finish(total + carry_ref[:, cols], old)

    @pl.when(jnp.logical_not(fits))
    def _():
        for j in range(keys // span):
            copy_out(step, j).wait()
        if not own:
            qaug_ref[3 * size : 3 * size + 16, cols] = jnp.where(extra_rows == 0, 1.0, 0.0).astype(
                BF
            )
        top = set_maximum(old)
        again = weigh()
        if not own:
            again = again + jnp.exp2(old - top) * carry_ref[:, cols]
        finish(again, top)

    @pl.when(step == pl.num_programs(0) - 1)
    def _():
        for at in range(kept_ref.shape[0]):
            for j in range(keys // span):
                copy_out(at, j).wait()


def forward_step(lane, beta, queries, kv, carry, last):
    sources, size, part = queries.shape
    count = sources * part
    block = count // 2
    own = carry is None
    vmem = pl.BlockSpec(memory_space=pltpu.VMEM)
    out_shape = (
        jax.ShapeDtypeStruct((count, count), BF),
        jax.ShapeDtypeStruct((48, count), F32),
    )
    if last:
        out_shape = out_shape[:1] + (jax.ShapeDtypeStruct((8, size, count // 8), BF),) + out_shape[1:]
    args = (lane.reshape(1), beta, queries, kv) + (() if own else (carry,))
    return pl.pallas_call(
        partial(forward_kernel, own=own, last=last, size=size, span=count // 8),
        grid=(count // block,),
        in_specs=[pl.BlockSpec(memory_space=pltpu.SMEM)] * 2 + [vmem] * (len(args) - 2),
        out_specs=(pl.BlockSpec(memory_space=pl.ANY),) + tuple(vmem for _ in out_shape[1:]),
        out_shape=out_shape,
        scratch_shapes=[
            pltpu.VMEM((4 * size, count), BF),
            pltpu.VMEM((count, 4 * size), BF),
            pltpu.VMEM((size + 16, count), BF),
            pltpu.VMEM((count // block, count, block), BF),
            pltpu.SemaphoreType.DMA((count // block, 8)),
        ],
        compiler_params=params(1),
        cost_estimate=pl.CostEstimate(
            flops=4 * count * count * 128, bytes_accessed=2**21, transcendentals=count * count
        ),
        name="sample_forward",
    )(*args)


def backward_kernel(
    lane_ref, q_ref, stat_ref, top_ref, do_ref, kv_ref, kept_ref, *rest, first, size, span, piece
):
    if first:
        held_ref = None
    else:
        held_ref, rest = rest[0], rest[1:]
    dq_ref, dkv_ref, factor_ref, daug_ref, vaug_ref, pside_ref, dside_ref, kt_ref = rest
    step = pl.program_id(0)
    block, count = kept_ref.shape

    @pl.when(step == 0)
    def _():
        keys = lay_rows(kv_ref, 0, size).astype(F32)
        kt_ref[...] = jnp.where(keys[0:1, :] > 0.5 * FLAG, 0.0, keys).astype(BF)
        row = lax.broadcasted_iota(jnp.int32, (size, count), 0)
        ones = jnp.where(row < 3, 1.0, 0.0).astype(BF)
        vaug_ref[...] = jnp.concatenate([lay_rows(kv_ref, size, 2 * size), ones], axis=0).T
        lanes = q_ref.shape[0]
        parts = do_ref.shape[0] // lanes
        grads = jnp.concatenate(
            [
                do_ref[(lane ^ lane_ref[0]) * parts + part]
                for lane in range(lanes)
                for part in range(parts)
            ],
            axis=1,
        ).astype(F32)
        delta = -jnp.sum(grads * stat_ref[0:size, :], axis=0, keepdims=True)
        extra = jnp.zeros((size, count), F32)
        for at, part in enumerate(three_parts(delta)):
            extra = jnp.where(row == at, part.astype(F32), extra)
        daug_ref[0:size, :] = grads.astype(BF)
        daug_ref[size : 2 * size, :] = extra.astype(BF)
        factor = jnp.exp2(top_ref[40:41, :] - stat_ref[size : size + 1, :])
        factor_ref[...] = jnp.broadcast_to(factor, factor_ref.shape)
        queries = lay_rows(q_ref, 0, size).astype(F32)
        pside_ref[...] = (grads * factor).astype(BF)
        dside_ref[...] = (queries * factor).astype(BF)
        dq_ref[...] = jnp.zeros(dq_ref.shape, F32)

    sums = [None] * (count // span)
    for i in range(block // piece):
        start = pl.multiple_of(step * block + i * piece, piece)
        rows = pl.ds(start, piece)
        dkeys = None
        for j in range(count // span):
            cols = slice(j * span, (j + 1) * span)
            prob = kept_ref[i * piece : (i + 1) * piece, cols]
            change = dot(vaug_ref[rows, :], daug_ref[:, cols])
            change = (prob.astype(F32) * change).astype(BF)
            terms = (
                dot_last(pside_ref[:, cols], prob),
                dot_last(dside_ref[:, cols], change),
            )
            dkeys = terms if dkeys is None else tuple(x + y for x, y in zip(dkeys, terms))
            term = dot(kt_ref[:, rows], change)
            sums[j] = term if sums[j] is None else sums[j] + term
        dkv_ref[0:size, rows] = dkeys[0].astype(dkv_ref.dtype)
        dkv_ref[size : 2 * size, rows] = dkeys[1].astype(dkv_ref.dtype)
    for j, term in enumerate(sums):
        dq_ref[:, j * span : (j + 1) * span] += term

    @pl.when(step == pl.num_programs(0) - 1)
    def _():
        total = dq_ref[...] * factor_ref[0:1, :]
        dq_ref[...] = total if first else total + held_ref[...]


def backward_step(lane, queries, stat, top, grads, kv, kept, held, kind):
    sources, size, part = queries.shape
    count = sources * part
    block = count // 4
    first = held is None
    vmem = pl.BlockSpec(memory_space=pltpu.VMEM)
    args = (lane.reshape(1), queries, stat, top, grads, kv, kept) + (() if first else (held,))
    return pl.pallas_call(
        partial(
            backward_kernel, first=first, size=size, span=count // 2, piece=count // 8
        ),
        grid=(count // block,),
        in_specs=[pl.BlockSpec(memory_space=pltpu.SMEM)]
        + [vmem] * 5
        + [pl.BlockSpec((block, count), lambda i: (i, 0))]
        + [vmem] * (len(args) - 7),
        out_specs=(vmem, vmem),
        out_shape=(
            jax.ShapeDtypeStruct((size, count), F32),
            jax.ShapeDtypeStruct((2 * size, count), kind),
        ),
        scratch_shapes=[
            pltpu.VMEM((8, count), F32),
            pltpu.VMEM((2 * size, count), BF),
            pltpu.VMEM((count, 2 * size), BF),
            pltpu.VMEM((size, count), BF),
            pltpu.VMEM((size, count), BF),
            pltpu.VMEM((size, count), BF),
        ],
        compiler_params=params(1),
        cost_estimate=pl.CostEstimate(
            flops=count * count * 128, bytes_accessed=2**20, transcendentals=0
        ),
        name="sample_backward",
    )(*args)


def lane_block(shape, block):
    return lax.broadcasted_iota(jnp.int32, shape, 1) // block


def to_tokens(rows8, turn_ref, base, entry):
    tiles = rows8.shape[1] // 128
    per_tile = 128 // entry
    where = lane_block((tiles, 128), entry)
    for j in range(tiles):
        turn_ref[base + j * GROUP : base + (j + 1) * GROUP, :] = rows8[:, j * 128 : (j + 1) * 128]
    by_row = [turn_ref[pl.ds(base + n, tiles, stride=GROUP), :] for n in range(GROUP)]
    strips = []
    for kk in range(per_tile):
        halves = []
        for quad in range(GROUP // per_tile):
            out = jnp.zeros((tiles, 128), F32)
            for i in range(per_tile):
                part = by_row[quad * per_tile + i]
                shift = ((i - kk) * entry) % 128
                if shift:
                    part = pltpu.roll(part, shift, 1)
                out = jnp.where(where == i, part, out)
            halves.append(out)
        strips.append(jnp.concatenate(halves, axis=1))
    return jnp.concatenate(strips, axis=0)


def from_tokens(block, turn_ref, base, entry):
    per_tile = 128 // entry
    tiles = block.shape[0] // per_tile
    where = lane_block((tiles, 128), entry)
    for n in range(GROUP):
        quad, i = divmod(n, per_tile)
        out = jnp.zeros((tiles, 128), F32)
        for kk in range(per_tile):
            part = block[kk * tiles : (kk + 1) * tiles, quad * 128 : (quad + 1) * 128]
            shift = ((kk - i) * entry) % 128
            if shift:
                part = pltpu.roll(part, shift, 1)
            out = jnp.where(where == kk, part, out)
        turn_ref[pl.ds(base + n, tiles, stride=GROUP), :] = out
    return jnp.concatenate(
        [turn_ref[base + j * GROUP : base + (j + 1) * GROUP, :] for j in range(tiles)], axis=1
    )


def heads_in_order(ret_ref, lanes, parts):
    return jnp.concatenate(
        [ret_ref[lane * parts + part] for part in range(parts) for lane in range(lanes)], axis=0
    )


def join_halves(mine_ref, theirs_ref, is_low):
    mine = mine_ref[...].astype(F32)
    theirs = theirs_ref[...].astype(F32)
    return jnp.concatenate(
        [jnp.where(is_low, mine, theirs), jnp.where(is_low, theirs, mine)], axis=1
    )


def turn_kernel_of(part_ref, cmine_ref, ctheirs_ref, c2_ref, turn_ref, *, entry):
    step_rows = cmine_ref.shape[0]
    upstream = join_halves(cmine_ref, ctheirs_ref, part_ref[0] == 0)
    tokens = upstream.shape[1] // entry
    area = upstream.shape[1] // 128 * GROUP
    for g in range(step_rows // GROUP):
        c2_ref[g * tokens : (g + 1) * tokens, :] = to_tokens(
            upstream[g * GROUP : (g + 1) * GROUP], turn_ref, g * area, entry
        ).astype(BF)


def enter_kernel(
    part_ref, x_ref, ret_ref, wout_ref, gain_ref, bias_ref,
    normed_ref, inverse_ref, t2_ref, rows_ref, turn_ref, *, lanes, parts, entry
):
    step = pl.program_id(0)
    step_rows, width = x_ref.shape
    area = width // 128 * GROUP
    tokens = width // entry

    @pl.when(step == 0)
    def _():
        rows_ref[...] = heads_in_order(ret_ref, lanes, parts).astype(F32).T.astype(BF)

    rows = pl.ds(pl.multiple_of(step * step_rows, step_rows), step_rows)
    hidden = x_ref[...].astype(F32) + dot(rows_ref[rows, :], wout_ref[...])
    centred = hidden - jnp.mean(hidden, axis=-1, keepdims=True)
    inverse = lax.rsqrt(jnp.mean(centred * centred, axis=-1, keepdims=True) + NORM_EPS)
    normed = centred * inverse
    normed_ref[...] = normed.astype(BF)
    inverse_ref[...] = jnp.broadcast_to(inverse, inverse_ref.shape)
    unit = normed * gain_ref[...] + bias_ref[...]
    for g in range(step_rows // GROUP):
        t2_ref[g * tokens : (g + 1) * tokens, :] = to_tokens(
            unit[g * GROUP : (g + 1) * GROUP], turn_ref, g * area, entry
        ).astype(BF)


def attend_kernel(
    beta_ref, t2_ref, c2_ref, pres_ref, wq_ref, wk_ref, wv_ref, wot_ref,
    back_ref, grad_ref, maps_ref,
    bm_ref, bn_ref, bm2_ref, bn2_ref, t2t_ref, c2t_ref, qn_ref, xn_ref, xq_ref, place_ref,
    tb_ref, sd_ref, pd_ref, zs_ref, un_ref, wn_ref, *, heads, size
):
    step = pl.program_id(0)
    _, tokens, _ = pres_ref.shape
    step_lanes, packed = t2_ref.shape
    entry = packed // GROUP
    assoc = heads * size
    lanes_all = heads * tokens
    tall = GROUP * tokens
    half_rows = tall // 2
    half_packed = packed // 2
    per_tile = 128 // entry
    part_lanes = 256

    @pl.when(step == 0)
    def _():
        owner = lax.broadcasted_iota(jnp.int32, (assoc, assoc), 0) // entry
        keep = lane_block((assoc, assoc), size) == owner

        def spread(weight_ref):
            tall_weight = jnp.concatenate([weight_ref[...].astype(F32)] * heads, axis=0)
            return jnp.where(keep, tall_weight, 0.0).astype(BF)

        score_map = dot_last(spread(wk_ref), jnp.concatenate([wq_ref[...]] * GROUP, axis=0))
        value_map = dot_last(spread(wv_ref), jnp.concatenate([wot_ref[...]] * GROUP, axis=0))
        place = lane_block((entry, packed), entry)
        for head in range(heads):
            score_rows = score_map[head * entry : (head + 1) * entry] * beta_ref[head]
            value_rows = value_map[head * entry : (head + 1) * entry]
            for n in range(GROUP):
                at = head * packed + n * entry
                bm2_ref[at : at + entry, :] = jnp.where(place == n, score_rows, 0.0).astype(BF)
                bn2_ref[at : at + entry, :] = jnp.where(place == n, value_rows, 0.0).astype(BF)
            span = slice(head * packed, (head + 1) * packed)
            bm_ref[:, span] = bm2_ref[span, :].astype(F32).T.astype(BF)
            bn_ref[:, span] = bn2_ref[span, :].astype(F32).T.astype(BF)
        row_place = lax.broadcasted_iota(jnp.int32, place_ref.shape, 0) // tokens
        place_ref[...] = jnp.where(
            row_place == lane_block(place_ref.shape, entry), 1.0, 0.0
        ).astype(BF)

    all_rows = pl.ds(pl.multiple_of(step * step_lanes, step_lanes), step_lanes)
    t2 = t2_ref[...]
    c2 = c2_ref[...]
    t2t_ref[:, all_rows] = t2.astype(F32).T.astype(BF)
    c2t_ref[:, all_rows] = c2.astype(F32).T.astype(BF)
    qn_ref[...] = dot(t2, bm_ref[...]).astype(BF)
    xn_ref[...] = dot(c2, bn_ref[...]).astype(BF)

    pair_lane = lax.broadcasted_iota(jnp.int32, (tokens, 128), 1) % tokens
    pair_row = lax.broadcasted_iota(jnp.int32, (tokens, 128), 0)
    diagonal = jnp.where(pair_lane == pair_row, 0.0, NEG)
    packed_place = lane_block((tokens, packed), entry)

    groups = step_lanes // tokens

    def score(g):
        own_rows = slice(g * tokens, (g + 1) * tokens)
        base = g * 2 * lanes_all
        for head in range(heads):
            cols = slice(head * packed, (head + 1) * packed)
            at = base + head * tokens
            xq_ref[at : at + tokens, :] = xn_ref[own_rows, cols]
            xq_ref[at + lanes_all : at + lanes_all + tokens, :] = qn_ref[own_rows, cols]
        tb = jnp.concatenate([t2[own_rows]] * GROUP, axis=0) * place_ref[...]
        rows = slice(g * tall, (g + 1) * tall)
        tb_ref[rows, :] = tb
        sd_ref[rows, :] = dot_last(tb, xq_ref[base : base + 2 * lanes_all, :])

    def soften(g):
        present = pres_ref[g]
        for n in range(GROUP):
            at = g * tall + n * tokens
            rows = slice(at, at + tokens)
            mask = jnp.maximum(diagonal, present[:, n : n + 1])
            mask = jnp.concatenate([mask] * (part_lanes // 128), axis=1)
            for part in range(lanes_all // part_lanes):
                span = slice(part * part_lanes, (part + 1) * part_lanes)
                far = slice(lanes_all + part * part_lanes, lanes_all + (part + 1) * part_lanes)
                own_scores = sd_ref[rows, far] + mask
                own_dprob = sd_ref[rows, span]
                terms = jnp.exp(own_scores - jnp.max(own_scores, axis=0, keepdims=True))
                prob = terms * (1.0 / jnp.sum(terms, axis=0, keepdims=True))
                delta = jnp.sum(prob * own_dprob, axis=0, keepdims=True)
                pd_ref[rows, span] = prob.astype(BF)
                pd_ref[rows, far] = (prob * (own_dprob - delta)).astype(BF)

    def gather(g):
        base = g * 2 * lanes_all
        at = g * tall
        tb_first = tb_ref[at : at + half_rows, 0:half_packed].astype(F32).T.astype(BF)
        tb_second = tb_ref[at + half_rows : at + tall, half_packed:].astype(F32).T.astype(BF)
        first_half = dot(tb_first, pd_ref[at : at + half_rows, :]).T.astype(BF)
        second_half = dot(tb_second, pd_ref[at + half_rows : at + tall, :]).T.astype(BF)
        group_rows = pl.ds(pl.multiple_of(step * step_lanes + g * tokens, tokens), tokens)
        for offset, target in ((0, un_ref), (lanes_all, wn_ref)):
            for head in range(heads):
                rows = slice(offset + head * tokens, offset + (head + 1) * tokens)
                cols = head * packed
                target[group_rows, cols : cols + half_packed] = first_half[rows]
                target[group_rows, cols + half_packed : cols + packed] = second_half[rows]
        side = xq_ref[base : base + 2 * lanes_all, :]
        halves = [
            dot(pd_ref[at : at + half_rows, :], side),
            dot(pd_ref[at + half_rows : at + tall, :], side),
        ]
        folded = jnp.zeros((tokens, packed), F32)
        for n in range(GROUP):
            half, row = divmod(n * tokens, half_rows)
            folded = jnp.where(packed_place == n, halves[half][row : row + tokens], folded)
        zs_ref[group_rows, :] = folded

    score(0)
    score(1)
    soften(0)
    for g in range(groups):
        if g + 2 < groups:
            score(g + 2)
        if g + 1 < groups:
            soften(g + 1)
        gather(g)

    @pl.when(step == pl.num_programs(0) - 1)
    def _():
        count = un_ref.shape[0] // 8
        for first in range(0, un_ref.shape[0], count):
            rows = slice(first, first + count)
            back_ref[rows, :] = dot(un_ref[rows, :], bn2_ref[...]).astype(BF)
            grad_ref[rows, :] = (zs_ref[rows, :] + dot(wn_ref[rows, :], bm2_ref[...])).astype(BF)
        value_sums = dot(c2t_ref[...], un_ref[...])
        score_sums = dot(t2t_ref[...], wn_ref[...])
        place = lane_block((entry, packed), entry)
        for d in range(heads):
            folded = []
            for acc in (value_sums, score_sums):
                total = jnp.zeros((entry, packed), F32)
                for n in range(GROUP):
                    piece = acc[n * entry : (n + 1) * entry, d * packed : (d + 1) * packed]
                    total = jnp.where(place == n, piece, total)
                total = total[:, 0:128] + total[:, 128:256]
                total = total + pltpu.roll(total, 64, 1)
                folded.append(total + pltpu.roll(total, 32, 1))
            where = lane_block((entry, 128), entry) == d % per_tile
            both = jnp.concatenate([jnp.where(where, total, 0.0) for total in folded], axis=1)
            maps_ref[d] = both.astype(BF)


def leave_kernel(
    part_ref, normed_ref, inverse_ref, gain_ref, bias_ref, cmine_ref, ctheirs_ref,
    back_ref, grad_ref, wout_ref,
    omine_ref, otheirs_ref, dh_ref, dret_ref, gain_acc, bias_acc, turn_ref,
    *, lanes, parts, entry
):
    step = pl.program_id(0)
    step_rows, width = normed_ref.shape
    area = width // 128 * GROUP
    tokens = width // entry
    half_width = width // parts

    @pl.when(step == 0)
    def _():
        gain_acc[...] = jnp.zeros(gain_acc.shape, F32)
        bias_acc[...] = jnp.zeros(bias_acc.shape, F32)

    is_low = part_ref[0] == 0
    changes = []
    token_grads = []
    for g in range(step_rows // GROUP):
        span = slice(g * tokens, (g + 1) * tokens)
        changes.append(from_tokens(back_ref[span, :].astype(F32), turn_ref, (2 * g) * area, entry))
        token_grads.append(from_tokens(grad_ref[span, :].astype(F32), turn_ref, (2 * g + 1) * area, entry))
    normed = normed_ref[...].astype(F32)
    gain = gain_ref[...]
    unit = normed * gain + bias_ref[...]
    out = (unit + jnp.concatenate(changes, axis=0)).astype(BF)
    low_out, high_out = out[:, :half_width], out[:, half_width:]
    omine_ref[...] = jnp.where(is_low, low_out, high_out)
    otheirs_ref[...] = jnp.where(is_low, high_out, low_out)
    dunit = join_halves(cmine_ref, ctheirs_ref, is_low) + jnp.concatenate(token_grads, axis=0)
    gain_acc[...] += jnp.sum(dunit * normed, axis=0, keepdims=True)
    bias_acc[...] += jnp.sum(dunit, axis=0, keepdims=True)
    dn = dunit * gain
    dhidden = inverse_ref[:, 0:1] * (
        dn
        - jnp.mean(dn, axis=-1, keepdims=True)
        - normed * jnp.mean(dn * normed, axis=-1, keepdims=True)
    )
    dh_ref[pl.ds(pl.multiple_of(step * step_rows, step_rows), step_rows), :] = dhidden.astype(BF)

    @pl.when(step == pl.num_programs(0) - 1)
    def _():
        size = dret_ref.shape[1]
        dret = dot_last(wout_ref[...], dh_ref[...]).astype(BF)
        for part in range(parts):
            for lane in range(lanes):
                head = part * lanes + lane
                dret_ref[lane * parts + part] = dret[head * size : (head + 1) * size]


def pack_kernel(ret_ref, dh_ref, gain_ref, bias_ref, maps_ref, pack_ref, *, lanes, parts):
    dests, _, cols = pack_ref.shape
    turned = heads_in_order(ret_ref, lanes, parts)
    assoc = turned.shape[0]
    out_grad = dot(turned, dh_ref[...]).astype(BF)
    row = lax.broadcasted_iota(jnp.int32, (16, cols), 0)
    for d in range(dests):
        span = slice(d * cols, (d + 1) * cols)
        pack_ref[d, 0:assoc, :] = out_grad[:, span]
        sums = jnp.where(row == 0, gain_ref[:, span], jnp.where(row == 1, bias_ref[:, span], 0.0))
        pack_ref[d, assoc : assoc + 16, :] = sums.astype(BF)
        pack_ref[d, assoc + 16 :, :] = maps_ref[d]


def make_pack(ret, dhidden, gain_sum, bias_sum, maps, parts):
    heads, size, _ = ret.shape
    entry = maps.shape[1]
    width = dhidden.shape[1]
    vmem = pl.BlockSpec(memory_space=pltpu.VMEM)
    return pl.pallas_call(
        partial(pack_kernel, lanes=heads // parts, parts=parts),
        in_specs=[vmem] * 5,
        out_specs=vmem,
        out_shape=jax.ShapeDtypeStruct((heads, heads * size + 16 + entry, width // heads), BF),
        compiler_params=params(),
        cost_estimate=pl.CostEstimate(flops=2**28, bytes_accessed=2**22, transcendentals=0),
        name="pack",
    )(ret, dhidden, gain_sum, bias_sum, maps)


def turn_cotangent(part, cot_mine, cot_theirs, parts, entry):
    half, half_width = cot_theirs.shape
    width = half_width * parts
    step_rows = GROUP * EDGE_GROUPS
    steps = half // step_rows
    step_lanes = EDGE_GROUPS * (width // entry)
    return pl.pallas_call(
        partial(turn_kernel_of, entry=entry),
        grid_spec=pltpu.PrefetchScalarGridSpec(
            num_scalar_prefetch=1,
            grid=(steps,),
            in_specs=[
                pl.BlockSpec((step_rows, half_width), lambda i, part: (part[0] * steps + i, 0)),
                pl.BlockSpec((step_rows, half_width), lambda i, part: (i, 0)),
            ],
            out_specs=pl.BlockSpec((step_lanes, GROUP * entry), lambda i, part: (i, 0)),
            scratch_shapes=[pltpu.VMEM((EDGE_GROUPS * (width // 128) * GROUP, 128), F32)],
        ),
        out_shape=jax.ShapeDtypeStruct((half // GROUP * (width // entry), GROUP * entry), BF),
        compiler_params=params(1),
        cost_estimate=pl.CostEstimate(flops=2**24, bytes_accessed=2**22, transcendentals=0),
        name="turn_cotangent",
    )(part.reshape(1), cot_mine, cot_theirs)


def middle(
    part_index, inputs, ret, w_out, gain, bias, cot_mine, cot_theirs, c2, present, feats, parts
):
    wq, wk, wv, wo, beta = feats
    rows, width = inputs.shape
    half = rows // parts
    heads, size, _ = ret.shape
    lanes = heads // parts
    tokens = present.shape[1]
    entry = width // tokens
    packed = GROUP * entry
    assoc = heads * size
    steps = half // (GROUP * STEP_GROUPS)
    edge_rows = GROUP * EDGE_GROUPS
    edge_steps = half // edge_rows
    edge_lanes = EDGE_GROUPS * tokens
    half_width = width // parts
    lanes_all = heads * tokens
    step_lanes = STEP_GROUPS * tokens
    all_lanes = half // GROUP * tokens
    vmem = pl.BlockSpec(memory_space=pltpu.VMEM)
    smem = pl.BlockSpec(memory_space=pltpu.SMEM)

    def own(shape):
        return pl.BlockSpec(shape, lambda i, part: (part[0] * edge_steps + i, 0))

    def stepped(shape):
        return pl.BlockSpec(shape, lambda i, *_: (i,) + (0,) * (len(shape) - 1))

    def array(shape, kind):
        return jax.ShapeDtypeStruct(shape, kind)

    part = part_index.reshape(1)
    gain = gain.reshape(1, width)
    bias = bias.reshape(1, width)
    turn = pltpu.VMEM((2 * EDGE_GROUPS * (width // 128) * GROUP, 128), F32)
    normed, inverse, t2 = pl.pallas_call(
        partial(enter_kernel, lanes=lanes, parts=parts, entry=entry),
        grid_spec=pltpu.PrefetchScalarGridSpec(
            num_scalar_prefetch=1,
            grid=(edge_steps,),
            in_specs=[own((edge_rows, width)), vmem, vmem, vmem, vmem],
            out_specs=[
                stepped((edge_rows, width)),
                stepped((edge_rows, 128)),
                stepped((edge_lanes, packed)),
            ],
            scratch_shapes=[pltpu.VMEM((half, assoc), BF), turn],
        ),
        out_shape=(
            array((half, width), BF),
            array((half, 128), F32),
            array((all_lanes, packed), BF),
        ),
        compiler_params=params(1),
        cost_estimate=pl.CostEstimate(flops=2**28, bytes_accessed=2**23, transcendentals=0),
        name="enter",
    )(part, inputs, ret, w_out, gain, bias)

    natural = pltpu.VMEM((all_lanes, heads * packed), BF)
    back, grad, maps = pl.pallas_call(
        partial(attend_kernel, heads=heads, size=size),
        grid=(steps,),
        in_specs=[
            smem,
            stepped((step_lanes, packed)),
            stepped((step_lanes, packed)),
            stepped((STEP_GROUPS, tokens, GROUP)),
            vmem,
            vmem,
            vmem,
            vmem,
        ],
        out_specs=[vmem, vmem, vmem],
        out_shape=(
            array((all_lanes, packed), BF),
            array((all_lanes, packed), BF),
            array((heads, entry, packed), BF),
        ),
        scratch_shapes=[
            pltpu.VMEM((packed, heads * packed), BF),
            pltpu.VMEM((packed, heads * packed), BF),
            pltpu.VMEM((heads * packed, packed), BF),
            pltpu.VMEM((heads * packed, packed), BF),
            pltpu.VMEM((packed, all_lanes), BF),
            pltpu.VMEM((packed, all_lanes), BF),
            pltpu.VMEM((step_lanes, heads * packed), BF),
            pltpu.VMEM((step_lanes, heads * packed), BF),
            pltpu.VMEM((STEP_GROUPS * 2 * lanes_all, packed), BF),
            pltpu.VMEM((GROUP * tokens, packed), BF),
            pltpu.VMEM((STEP_GROUPS * GROUP * tokens, packed), BF),
            pltpu.VMEM((STEP_GROUPS * GROUP * tokens, 2 * lanes_all), F32),
            pltpu.VMEM((STEP_GROUPS * GROUP * tokens, 2 * lanes_all), BF),
            pltpu.VMEM((all_lanes, packed), F32),
            natural,
            natural,
        ],
        compiler_params=params(1),
        cost_estimate=pl.CostEstimate(
            flops=2 * 1200 * half * 256 * 256,
            bytes_accessed=2**23,
            transcendentals=half * heads * tokens * tokens,
        ),
        name="attend",
    )(beta, t2, c2, present, wq, wk, wv, wo)

    out_mine, out_theirs, dhidden, dret, gain_sum, bias_sum = pl.pallas_call(
        partial(leave_kernel, lanes=lanes, parts=parts, entry=entry),
        grid_spec=pltpu.PrefetchScalarGridSpec(
            num_scalar_prefetch=1,
            grid=(edge_steps,),
            in_specs=[
                stepped((edge_rows, width)),
                stepped((edge_rows, 128)),
                vmem,
                vmem,
                own((edge_rows, half_width)),
                stepped((edge_rows, half_width)),
                stepped((edge_lanes, packed)),
                stepped((edge_lanes, packed)),
                vmem,
            ],
            out_specs=[
                stepped((edge_rows, half_width)),
                stepped((edge_rows, half_width)),
                vmem,
                vmem,
                vmem,
                vmem,
            ],
            scratch_shapes=[turn],
        ),
        out_shape=(
            array((half, half_width), BF),
            array((half, half_width), BF),
            array((half, width), BF),
            array((heads, size, half), BF),
            array((1, width), F32),
            array((1, width), F32),
        ),
        compiler_params=params(1),
        cost_estimate=pl.CostEstimate(flops=2**28, bytes_accessed=2**23, transcendentals=0),
        name="leave",
    )(part, normed, inverse, gain, bias, cot_mine, cot_theirs, back, grad, w_out)
    return out_mine, out_theirs, dhidden, dret, gain_sum, bias_sum, maps


def weight_grad_kernel(
    place_ref, beta_ref, dq_ref, term_ref, moved_ref, x_ref, rows_ref, *rest, size
):
    outs, (whole_ref, joined_ref) = rest[:-2], rest[-2:]
    step = pl.program_id(0)
    rows = rows_ref.shape[2]
    lanes = joined_ref.shape[1] // rows
    parts = rows_ref.shape[0] // lanes
    width = x_ref.shape[1]

    @pl.when(step == 0)
    def _():
        beta = beta_ref[0]
        dkv = term_ref[...] + moved_ref[...].astype(F32)
        joined = jnp.concatenate([dq_ref[...] * beta, dkv[size:] * beta, dkv[:size]], axis=0)
        joined = joined.astype(BF)
        for relative in range(lanes):
            block = joined[:, relative * rows : (relative + 1) * rows]
            other = relative ^ place_ref[0]
            joined_ref[:, pl.ds(pl.multiple_of(other * rows, rows), rows)] = block
            for part in range(parts):
                rows_ref[other * parts + part] = block

    product = dot(joined_ref[...], x_ref[...]).astype(BF)
    whole_ref[:, pl.ds(pl.multiple_of(step * width, width), width)] = product

    @pl.when(step == pl.num_programs(0) - 1)
    def _():
        slabs, _, piece = outs[0].shape if len(outs) == 1 else (len(outs),) + outs[0].shape
        for r in range(slabs):
            if len(outs) == 1:
                outs[0][r ^ place_ref[2]] = whole_ref[:, r * piece : (r + 1) * piece]
            else:
                start = pl.multiple_of((r ^ place_ref[2]) * piece, piece)
                outs[r][...] = whole_ref[:, pl.ds(start, piece)]


def weight_grads(place, beta, dq, term, moved, slab_inputs, lanes, slabs, parts):
    size = dq.shape[0]
    three = 3 * size
    total, width = slab_inputs.shape
    rows = total // lanes
    piece = width // slabs
    vmem = pl.BlockSpec(memory_space=pltpu.VMEM)
    smem = pl.BlockSpec(memory_space=pltpu.SMEM)
    if piece % 128:
        shapes = [jax.ShapeDtypeStruct((slabs, three, piece), BF)]
    else:
        shapes = [jax.ShapeDtypeStruct((three, piece), BF)] * slabs
    dqkv_rows, *grads = pl.pallas_call(
        partial(weight_grad_kernel, size=size),
        grid=(2,),
        in_specs=[smem, smem, vmem, vmem, vmem]
        + [pl.BlockSpec((total, width // 2), lambda i: (0, i))],
        out_specs=[vmem] * (1 + len(shapes)),
        out_shape=[jax.ShapeDtypeStruct((lanes * parts, three, rows), BF)] + shapes,
        scratch_shapes=[pltpu.VMEM((three, width), BF), pltpu.VMEM((three, total), BF)],
        compiler_params=params(1),
        cost_estimate=pl.CostEstimate(flops=2**20, bytes_accessed=2**16, transcendentals=0),
        name="weight_grads",
    )(place, beta, dq, term, moved, slab_inputs)
    return dqkv_rows, grads[0] if piece % 128 else grads


def input_grad_kernel(
    place_ref, x_ref, *rest, lanes, size
):
    wm_ref, wt_ref, dm_ref, du_ref, dl_ref, out_ref, mine_ref, theirs_ref = rest
    part = place_ref[1]
    parts = x_ref.shape[0] // lanes

    @pl.when(pl.program_id(0) == 0)
    def _():
        for source, target in ((part, mine_ref), (parts - 1 - part, theirs_ref)):
            blocks = [
                x_ref[lane * parts + source, kind * size : (kind + 1) * size, :]
                for kind in range(3)
                for lane in range(lanes)
            ]
            target[...] = jnp.concatenate(blocks, axis=0).T

    wm = jnp.concatenate([wm_ref[kind] for kind in range(3)], axis=1)
    wt = jnp.concatenate([wt_ref[kind] for kind in range(3)], axis=1)
    out = dot_last(mine_ref[...], wm) + dot_last(theirs_ref[...], wt)
    half = dm_ref.shape[0]
    mine = dm_ref[...].astype(F32)
    theirs = jnp.concatenate([du_ref[...], dl_ref[...]], axis=0).astype(F32)
    is_low = part == 0
    out_ref[0:half, :] = (out[0:half] + jnp.where(is_low, mine, theirs)).astype(BF)
    out_ref[half:, :] = (out[half:] + jnp.where(is_low, theirs, mine)).astype(BF)


def input_grads(place, dqkv_rows, w_mine, w_theirs, dh_mine, dh_upper, dh_lower, lanes):
    _, three, rows = dqkv_rows.shape
    _, width, local = w_mine.shape
    half = dh_mine.shape[0]
    block = width // 2
    weight = pl.BlockSpec((3, block, local), lambda i: (0, i, 0))
    residual = pl.BlockSpec((half, block), lambda i: (0, i))
    return pl.pallas_call(
        partial(input_grad_kernel, lanes=lanes, size=three // 3),
        grid=(width // block,),
        in_specs=[
            pl.BlockSpec(memory_space=pltpu.SMEM),
            pl.BlockSpec(memory_space=pltpu.VMEM),
        ]
        + [weight] * 2
        + [residual]
        + [pl.BlockSpec((half // 2, block), lambda i: (0, i))] * 2,
        out_specs=pl.BlockSpec((rows, block), lambda i: (0, i)),
        out_shape=jax.ShapeDtypeStruct((rows, width), BF),
        scratch_shapes=[pltpu.VMEM((rows, 3 * local), BF)] * 2,
        compiler_params=params(1),
        cost_estimate=pl.CostEstimate(flops=2**20, bytes_accessed=2**16, transcendentals=0),
        name="input_grads",
    )(place, dqkv_rows, w_mine, w_theirs, dh_mine, dh_upper, dh_lower)


def turn_kernel(place_ref, beta_ref, *rest, size):
    kinds, rest = rest[:4], rest[4:]
    wq_ref, gq_ref, gk_ref, gv_ref, sum_ref, acc_ref, hold_ref = rest
    step = pl.program_id(0)
    for kind, kind_ref in enumerate(kinds):
        hold_ref[kind] = kind_ref[0]

    side, odd = place_ref[0] // 2, place_ref[0] % 2
    pieces = [
        hold_ref[2 * ((lane % 2) ^ odd) + ((lane // 2) ^ side)].astype(F32) for lane in range(4)
    ]
    for place, target in enumerate((gq_ref, gk_ref, gv_ref)):
        target[...] = jnp.concatenate(
            [piece[place * size : (place + 1) * size] for piece in pieces], axis=0
        ).T
    product = jnp.sum(gq_ref[...] * wq_ref[...].astype(F32), axis=0, keepdims=True)

    @pl.when(step == 0)
    def _():
        acc_ref[...] = product

    @pl.when(step > 0)
    def _():
        acc_ref[...] += product

    @pl.when(step == pl.num_programs(0) - 1)
    def _():
        total = acc_ref[...]
        owner = lane_block(total.shape, size)
        at = lax.broadcasted_iota(jnp.int32, (1, 128), 1)
        sums = jnp.zeros((1, 128), F32)
        for lane in range(len(pieces)):
            own = jnp.sum(jnp.where(owner == lane, total, 0.0), axis=1, keepdims=True)
            sums = jnp.where(at == lane, own / beta_ref[lane], sums)
        sum_ref[...] = sums[:, 0 : len(pieces)]


def turn_grads(place, beta, blocks, w_query):
    slabs, three, piece = blocks[0].shape
    lanes = len(blocks)
    size = three // 3
    source = pl.BlockSpec((1, three, piece), lambda i, at: (i ^ at[2], 0, 0))
    target = pl.BlockSpec((piece, lanes * size), lambda i, at: (i, 0))
    shape = jax.ShapeDtypeStruct((slabs * piece, lanes * size), F32)
    return pl.pallas_call(
        partial(turn_kernel, size=size),
        grid_spec=pltpu.PrefetchScalarGridSpec(
            num_scalar_prefetch=1,
            grid=(slabs,),
            in_specs=[pl.BlockSpec(memory_space=pltpu.SMEM)] + [source] * lanes + [target],
            out_specs=[target, target, target, pl.BlockSpec((1, lanes), lambda i, at: (0, 0))],
            scratch_shapes=[
                pltpu.VMEM((1, lanes * size), F32),
                pltpu.VMEM((lanes, three, piece), BF),
            ],
        ),
        out_shape=(shape, shape, shape, jax.ShapeDtypeStruct((1, lanes), F32)),
        compiler_params=params(1),
        cost_estimate=pl.CostEstimate(flops=0, bytes_accessed=2**16, transcendentals=0),
        name="turn_grads",
    )(place, beta, *blocks, w_query)


def unpack_kernel(
    place_ref, beta_ref, near_ref, far_ref, wq_ref, wk_ref, wv_ref, wo_ref,
    out_ref, gain_ref, bias_ref, fq_ref, fk_ref, fv_ref, fo_ref, fb_ref, *, size
):
    parts, sides, _, cols = near_ref.shape
    heads = 2 * sides * parts
    assoc = heads * size
    entry = wq_ref.shape[0]
    side, even, part = place_ref[0] // 2, place_ref[0] % 2 == 0, place_ref[1]
    per_tile = 128 // entry
    tiles = heads // per_tile
    maps = [[jnp.zeros((entry, 128), F32) for _ in range(tiles)] for _ in range(4)]
    for d in range(heads):
        lane, of_part = divmod(d, parts)
        of_side, odd = divmod(lane, 2)
        at_part = (of_part + part) % parts
        at_side = (of_side + side) % sides
        near = near_ref[at_part, at_side].astype(F32)
        far = far_ref[at_part, at_side].astype(F32)
        whole = jnp.where(even, far if odd else near, near if odd else far)
        span = slice(d * cols, (d + 1) * cols)
        out_ref[:, span] = whole[0:assoc]
        gain_ref[:, span] = whole[assoc : assoc + 1]
        bias_ref[:, span] = whole[assoc + 1 : assoc + 2]
        block = whole[assoc + 16 : assoc + 16 + entry]
        tile, slot = divmod(d, per_tile)
        for kind in range(2):
            piece = block[:, kind * 128 : (kind + 1) * 128]
            square = jnp.concatenate([piece, jnp.zeros((128 - entry, 128), F32)], axis=0).T
            turned = square[slot * entry : (slot + 1) * entry]
            if slot:
                turned = pltpu.roll(turned, slot * entry, 1)
            maps[2 * kind][tile] = maps[2 * kind][tile] + piece
            maps[2 * kind + 1][tile] = maps[2 * kind + 1][tile] + turned
    value_turned, value, score_turned, score = [
        jnp.concatenate(tile_list, axis=1).astype(BF) for tile_list in maps
    ]
    lane = lax.broadcasted_iota(jnp.int32, (assoc, assoc), 1) // size
    owner = lax.broadcasted_iota(jnp.int32, (assoc, assoc), 0) // entry

    def spread(weights):
        tall = jnp.concatenate([weights.astype(F32)] * heads, axis=0)
        return jnp.where(lane == owner, tall, 0.0).astype(BF)

    scale = jnp.zeros((1, assoc), F32)
    for head in range(heads):
        scale = jnp.where(lane[0:1] == head, beta_ref[head], scale)
    fq = dot(score_turned, spread(wk_ref[...]))
    fq_ref[...] = fq * scale
    fk_ref[...] = dot(score, spread(wq_ref[...])) * scale
    fv_ref[...] = dot(value, spread(wo_ref[...]))
    fo_ref[...] = dot(value_turned, spread(wv_ref[...]))
    sums = jnp.sum(fq * wq_ref[...].astype(F32), axis=0, keepdims=True)
    at = lax.broadcasted_iota(jnp.int32, (1, 128), 1)
    each = jnp.zeros((1, 128), F32)
    for head in range(heads):
        own = jnp.sum(jnp.where(lane[0:1] == head, sums, 0.0), axis=1, keepdims=True)
        each = jnp.where(at == head, own, each)
    fb_ref[...] = each[:, 0:heads]


def unpack(place, beta, near, far, wq, wk, wv, wo, size):
    parts, sides, _, cols = near.shape
    heads = 2 * sides * parts
    width = heads * cols
    vmem = pl.BlockSpec(memory_space=pltpu.VMEM)
    smem = pl.BlockSpec(memory_space=pltpu.SMEM)
    shapes = [(heads * size, width), (1, width), (1, width)]
    shapes += [wq.shape, wk.shape, wv.shape, wo.shape, (1, heads)]
    return pl.pallas_call(
        partial(unpack_kernel, size=size),
        in_specs=[smem, smem] + [vmem] * 6,
        out_specs=tuple(vmem for _ in shapes),
        out_shape=tuple(jax.ShapeDtypeStruct(shape, F32) for shape in shapes),
        compiler_params=params(),
        cost_estimate=pl.CostEstimate(flops=2**20, bytes_accessed=2**16, transcendentals=0),
        name="unpack",
    )(place, beta, near, far, wq, wk, wv, wo)


def tie(*values):
    return lax.optimization_barrier(values)


def body(
    inputs,
    memory_keep,
    feature_present,
    w_query,
    w_key,
    w_value,
    beta_sample,
    w_out,
    norm_gain,
    norm_bias,
    wf_query,
    wf_key,
    wf_value,
    beta_feature,
    wf_out,
    cotangent,
):
    rows, width = inputs.shape
    lanes = beta_sample.shape[0]
    parts = lax.axis_size("heads")
    slabs = lax.axis_size("slab")
    lane = lax.axis_index("lane")
    part = lax.axis_index("heads")
    half = rows // parts
    size = w_query.shape[1] // lanes
    tokens = feature_present.shape[1]
    entry = width // tokens
    heads = lanes * parts
    flip = [(i, (i + 1) % parts) for i in range(parts)]
    ring = [(i, (i + 1) % slabs) for i in range(slabs)]
    group = ("lane", "heads")

    def spread(x, axes):
        return lax.all_to_all(x, axes, split_axis=0, concat_axis=0, tiled=True)

    place = jnp.stack([lane, part, lax.axis_index("slab")]).astype(jnp.int32)

    def swap(x, axes, count, bits):
        return lax.ppermute(x, axes, [(i, i ^ bits) for i in range(count)])

    *pieces, weights_mine = project(
        lane, inputs, w_query, w_key, w_value, memory_keep, lanes
    )
    pieces = [pieces[0]] + [swap(pieces[r], "lane", lanes, r) for r in range(1, lanes)]
    queries = jnp.stack([piece[:size] for piece in pieces])
    beta = lax.dynamic_slice_in_dim(beta_sample, lane, 1, 0)

    held = [jnp.stack([piece[size:] for piece in pieces])]
    kept = []
    tops = []
    carry = None
    for step in range(slabs):
        if step + 1 < slabs:
            held.append(lax.ppermute(held[-1], "slab", ring))
        outs = forward_step(lane, beta, queries, held[step], carry, step + 1 == slabs)
        kept.append(outs[0])
        carry = outs[-1]
        tops.append(carry)
        if step + 1 < slabs:
            held[-1], carry = tie(held[-1], carry)
        if step == 0:
            carry, inputs_late, cot_late = tie(carry, inputs, cotangent)
            slab_inputs = lax.all_gather(inputs_late, "lane", axis=0, tiled=True)
            other_start = (parts - 1 - part) * half
            cot_theirs = lax.ppermute(
                lax.dynamic_slice_in_dim(cot_late, other_start, half, 0), "heads", flip
            )
    _, ret, stat = outs
    ret = spread(ret, group)
    c2 = turn_cotangent(part, cotangent, cot_theirs, parts, entry)
    ret, c2, weights_mine = tie(ret, c2, weights_mine)
    weights_theirs = lax.ppermute(weights_mine, "heads", flip)

    own_present = lax.dynamic_slice_in_dim(feature_present, part * half, half, 0)
    present = own_present.reshape(half // GROUP, GROUP, tokens * entry // 128, 128 // entry)
    present = present.transpose(0, 3, 2, 1).reshape(half // GROUP, tokens, GROUP)
    present = jnp.where(present > 0, 0.0, NEG).astype(F32)
    feats = (wf_query, wf_key, wf_value, wf_out.T, beta_feature)
    out_mine, out_theirs, dhidden, dret, gain_sum, bias_sum, maps = middle(
        part,
        inputs,
        ret,
        w_out,
        norm_gain,
        norm_bias,
        cotangent,
        cot_theirs,
        c2,
        present,
        feats,
        parts,
    )
    dret = spread(dret, group)
    pack = make_pack(ret, dhidden, gain_sum, bias_sum, maps, parts)
    pack, dret, weights_theirs = tie(pack, dret, weights_theirs)
    pack = spread(pack, group)

    dq = None
    moved = None
    bit = 1
    for step in range(slabs):
        at = (step + 1) % slabs
        last = step + 1 == slabs
        dq, term = backward_step(
            lane, queries, stat, tops[at], dret, held[at], kept[at], dq, F32 if last else BF
        )
        if last:
            break
        total = term if moved is None else (term.astype(F32) + moved.astype(F32)).astype(BF)
        total, dq = tie(total, dq)
        moved = lax.ppermute(total, "slab", ring)
        if step == 0:
            upper, dq = tie(dhidden[: half // 2], dq)
            upper = lax.ppermute(upper, "heads", flip)
        elif step == 1:
            upper, lower, dq = tie(upper, dhidden[half // 2 :], dq)
            lower = lax.ppermute(lower, "heads", flip)
        elif step == 2:
            lower, out_theirs, dq = tie(lower, out_theirs, dq)
            out_other = lax.ppermute(out_theirs, "heads", flip)
        if step == 1:
            pack, dq = tie(pack.astype(F32).sum(axis=0).astype(BF), dq)
        elif step > 1 and bit < slabs:
            pack, dq = tie((pack.astype(F32) + pack_other.astype(F32)).astype(BF), dq)
            bit *= 2
        if step > 0 and bit < slabs:
            pack_other = swap(pack, "slab", slabs, bit)
    term, out_other = tie(term, out_other)
    if bit < slabs:
        term, pack_other = tie(term, pack_other)

    dqkv_rows, grads = weight_grads(
        place, beta, dq, term, moved, slab_inputs, lanes, slabs, parts
    )
    if bit < slabs:
        pack, pack_other, dqkv_rows = tie(pack, pack_other, dqkv_rows)
        pack = (pack.astype(F32) + pack_other.astype(F32)).astype(BF)
    terms = [grads[0]] + [swap(grads[r], "slab", slabs, r) for r in range(1, slabs)]
    terms[1], dqkv_rows = tie(terms[1], dqkv_rows)
    dqkv_rows = spread(dqkv_rows, group)
    grads = sum(term.astype(F32) for term in terms).astype(BF)
    grads = jnp.stack([grads] + [swap(grads, "slab", slabs, r) for r in range(1, slabs)])
    far = swap(grads, "lane", lanes, lanes // 2)
    near = swap(grads, "lane", lanes, 1)
    pack, dqkv_rows = tie(pack, dqkv_rows)
    pack_far = [swap(pack, group, heads, bits) for bits in (1, heads // 2, heads // 2 + 1)]
    pack = jnp.stack([jnp.stack([pack, pack_far[1]]), jnp.stack([pack_far[0], pack_far[2]])])
    pack_near = swap(pack, "lane", lanes, 1)
    sum_out, sum_gain, sum_bias, sum_fquery, sum_fkey, sum_fvalue, sum_fout, fbeta = unpack(
        place, beta_feature, pack, pack_near, wf_query, wf_key, wf_value, wf_out.T, size
    )
    input_grad = input_grads(
        place, dqkv_rows, weights_mine, weights_theirs, dhidden, upper, lower, lanes
    )
    is_low = part == 0
    block_out = jnp.concatenate(
        [jnp.where(is_low, out_mine, out_other), jnp.where(is_low, out_other, out_mine)], axis=0
    )
    far, input_grad, block_out, near = tie(far, input_grad, block_out, near)
    near_far = swap(far, "lane", lanes, 1)
    sum_wquery, sum_wkey, sum_wvalue, sums = turn_grads(
        place, beta_sample, [grads, far, near, near_far], w_query
    )
    return (
        block_out,
        input_grad,
        sum_wquery,
        sum_wkey,
        sum_wvalue,
        sums.reshape(lanes),
        sum_out,
        sum_gain.reshape(width),
        sum_bias.reshape(width),
        sum_fquery,
        sum_fkey,
        sum_fvalue,
        fbeta.reshape(heads),
        sum_fout.T,
    )


def solution(mesh):
    parts = mesh.shape["heads"]
    lanes = 8 // parts
    fine = Mesh(mesh.devices.reshape(-1, lanes, parts), ("slab", "lane", "heads"))
    rows = ("slab", "lane")
    in_specs = (
        P(rows, None),
        P(rows),
        P(rows, None),
        P(None, "heads"),
        P(None, "heads"),
        P(None, "heads"),
        P("heads"),
        P(),
        P(),
        P(),
        P(),
        P(),
        P(),
        P(),
        P(),
        P(rows, "heads"),
    )
    out_specs = (
        P(rows, "heads"),
        P(rows, None),
        P(None, "heads"),
        P(None, "heads"),
        P(None, "heads"),
        P("heads"),
        P(),
        P(),
        P(),
        P(),
        P(),
        P(),
        P(),
        P(),
    )
    return jax.shard_map(body, mesh=fine, in_specs=in_specs, out_specs=out_specs, check_vma=False)
```

```python
from functools import partial

import jax
import jax.numpy as jnp
from jax import lax
from jax.experimental import pallas as pl
from jax.experimental.pallas import tpu as pltpu
from jax.sharding import Mesh, PartitionSpec as P

BF = jnp.bfloat16
F32 = jnp.float32
NEG = -1e30
FLAG = 1e30
NORM_EPS = 1e-05
LOG2E = 1.4426950408889634
SUM_LIMIT = 2.0**60
VMEM_BYTES = 56 * 1024 * 1024
GROUP = 8
STEP_GROUPS = 4
EDGE_GROUPS = 8


def dot(a, b):
    return jnp.dot(a, b, preferred_element_type=F32)


def dot_last(a, b):
    return lax.dot_general(a, b, (((1,), (1,)), ((), ())), preferred_element_type=F32)


def split_dot(a, b_ref, pieces):
    depth = a.shape[1] // pieces
    terms = [
        dot(a[:, j * depth : (j + 1) * depth], b_ref[j * depth : (j + 1) * depth, :])
        for j in range(pieces)
    ]
    while len(terms) > 1:
        terms = [x + y for x, y in zip(terms[::2], terms[1::2])]
    return terms[0]


def params(steps=0):
    return pltpu.CompilerParams(
        vmem_limit_bytes=VMEM_BYTES,
        dimension_semantics=("arbitrary",) * steps if steps else None,
    )


def three_parts(x):
    high = x.astype(BF)
    rest = x - high.astype(F32)
    mid = rest.astype(BF)
    low = (rest - mid.astype(F32)).astype(BF)
    return high, mid, low


def project_kernel(lane_ref, x_ref, wq_ref, wk_ref, wv_ref, keep_ref, *rest):
    *outs, joined_ref, turned_ref, sem = rest
    copies = [
        pltpu.make_async_copy(w_ref, joined_ref.at[place], sem.at[place])
        for place, w_ref in enumerate((wq_ref, wk_ref, wv_ref))
    ]

    @pl.when(pl.program_id(0) == 0)
    def _():
        for copy in copies:
            copy.start()

    rows3, _ = outs[0].shape
    size = rows3 // 3
    x = x_ref[...]
    for place, w_ref in enumerate((wq_ref, wk_ref, wv_ref)):
        turned = split_dot(x, w_ref, 4).T
        if place == 1:
            turned = jnp.where(keep_ref[...] > 0, turned, FLAG)
        turned_ref[...] = turned
        for relative, out_ref in enumerate(outs):
            head = pl.multiple_of((lane_ref[0] ^ relative) * size, size)
            out_ref[place * size : (place + 1) * size, :] = turned_ref[pl.ds(head, size), :].astype(
                BF
            )

    @pl.when(pl.program_id(0) == pl.num_programs(0) - 1)
    def _():
        for copy in copies:
            copy.wait()


def project(lane, inputs, w_query, w_key, w_value, keep, heads):
    rows, width = inputs.shape
    local = w_query.shape[1]
    size = local // heads
    block = min(rows, 256)
    weight = pl.BlockSpec(memory_space=pltpu.VMEM)
    return pl.pallas_call(
        project_kernel,
        grid=(rows // block,),
        in_specs=[
            pl.BlockSpec(memory_space=pltpu.SMEM),
            pl.BlockSpec((block, width), lambda i: (i, 0)),
            weight,
            weight,
            weight,
            pl.BlockSpec((1, block), lambda i: (0, i)),
        ],
        out_specs=[pl.BlockSpec((3 * size, block), lambda i: (0, i))] * heads
        + [pl.BlockSpec(memory_space=pl.ANY)],
        out_shape=[jax.ShapeDtypeStruct((3 * size, rows), BF)] * heads
        + [jax.ShapeDtypeStruct((3, width, local), BF)],
        scratch_shapes=[pltpu.VMEM((local, block), F32), pltpu.SemaphoreType.DMA((3,))],
        compiler_params=params(1),
        cost_estimate=pl.CostEstimate(
            flops=6 * rows * width * local,
            bytes_accessed=2 * (rows * width + 3 * width * local),
            transcendentals=0,
        ),
        name="project",
    )(lane.reshape(1), inputs, w_query, w_key, w_value, keep.reshape(1, rows))


def lay_rows(ref, first, last):
    return jnp.concatenate([ref[s, first:last, :] for s in range(ref.shape[0])], axis=1)


def build_keys(kv_ref, kaug_ref, size):
    keys = lay_rows(kv_ref, 0, size).astype(F32)
    flagged = keys[0:1, :] > 0.5 * FLAG
    clean = jnp.where(flagged, 0.0, keys)
    count = keys.shape[1]
    row = lax.broadcasted_iota(jnp.int32, (size, count), 0)
    bias = jnp.where(flagged, NEG, 0.0)
    extra = jnp.where(row == 0, bias, jnp.where(row < 4, 1.0, 0.0))
    clean = clean.astype(BF)
    kaug_ref[...] = jnp.concatenate([clean, clean, clean, extra.astype(BF)], axis=0).T


def build_queries(beta, q_ref, qaug_ref, size):
    queries = lay_rows(q_ref, 0, size).astype(F32) * (beta * LOG2E)
    row = lax.broadcasted_iota(jnp.int32, queries.shape, 0)
    high, mid, low = three_parts(queries)
    qaug_ref[0:size, :] = high
    qaug_ref[size : 2 * size, :] = mid
    qaug_ref[2 * size : 3 * size, :] = low
    qaug_ref[3 * size : 4 * size, :] = jnp.where(row == 0, 1.0, 0.0).astype(BF)


def hide_own(scores, first_key, first_query):
    key = lax.broadcasted_iota(jnp.int32, scores.shape, 0) + first_key
    query = lax.broadcasted_iota(jnp.int32, scores.shape, 1) + first_query
    return jnp.where(key == query, NEG, scores)


def forward_kernel(lane_ref, beta_ref, q_ref, kv_ref, *rest, own, last, size, span):
    if own:
        carry_ref = None
    else:
        carry_ref, rest = rest[0], rest[1:]
    far_ref, *outs = rest[:-5]
    qaug_ref, kaug_ref, vaug_ref, kept_ref, sem = rest[-5:]
    step = pl.program_id(0)
    keys, block = kept_ref.shape[1:]

    @pl.when(step == 0)
    def _():
        build_keys(kv_ref, kaug_ref, size)
        build_queries(beta_ref[0], q_ref, qaug_ref, size)
        vaug_ref[0:size, :] = lay_rows(kv_ref, size, 2 * size)
        row = lax.broadcasted_iota(jnp.int32, (16, keys), 0)
        vaug_ref[size : size + 16, :] = jnp.where(row == 0, 1.0, 0.0).astype(BF)

    cols = pl.ds(pl.multiple_of(step * block, block), block)
    extra_rows = lax.broadcasted_iota(jnp.int32, (16, block), 0)

    def scores_of(j):
        scores = dot(kaug_ref[j * span : (j + 1) * span, :], qaug_ref[:, cols])
        if own:
            scores = hide_own(scores, j * span, step * block)
        return scores

    def set_shift(shift):
        extra = jnp.where(extra_rows == 0, 1.0, 0.0)
        for row, part in enumerate(three_parts(-shift)):
            extra = jnp.where(extra_rows == row + 1, part.astype(F32), extra)
        qaug_ref[3 * size : 3 * size + 16, cols] = extra.astype(BF)

    def set_maximum(least):
        tops = jnp.full((8, block), 2 * NEG, F32)
        for j in range(keys // span):
            tops = jnp.maximum(tops, jnp.max(scores_of(j).reshape(span // 8, 8, block), axis=0))
        top = jnp.max(tops, axis=0, keepdims=True)
        if least is not None:
            top = jnp.maximum(top, least)
        set_shift(top)
        return top

    def copy_out(at, j):
        rows = slice(j * span, (j + 1) * span)
        lanes = pl.ds(pl.multiple_of(at * block, block), block)
        return pltpu.make_async_copy(
            kept_ref.at[at, rows, :], far_ref.at[rows, lanes], sem.at[at, j]
        )

    def weigh():
        count = keys // span
        half = count // 2
        ahead = scores_of(0)
        total = None
        for j in range(count):
            scores = ahead
            if j + 1 < count:
                ahead = scores_of(j + 1)
            if j == half + 2:
                total = dot(vaug_ref[:, : half * span], kept_ref[step, : half * span, :])
            kept_ref[step, j * span : (j + 1) * span, :] = jnp.exp2(scores).astype(BF)
            copy_out(step, j).start()
        return total + dot(vaug_ref[:, half * span :], kept_ref[step, half * span :, :])

    stat_ref = outs[-1]

    def finish(total, top):
        if last:
            ret_ref = outs[0]
            summed = total[size : size + 1, :]
            result = total[0:size, :] / summed
            places, _, piece = ret_ref.shape
            parts = places // q_ref.shape[0]
            for j in range(block // piece):
                lane = (step * (block // piece // parts) + j // parts) ^ lane_ref[0]
                ret_ref[lane * parts + j % parts] = result[:, j * piece : (j + 1) * piece].astype(BF)
            stat_ref[0:size, cols] = result
            stat_ref[size : size + 8, cols] = jnp.broadcast_to(top + jnp.log2(summed), (8, block))
        else:
            stat_ref[0:40, cols] = total[0:40, :]
        stat_ref[40:48, cols] = jnp.broadcast_to(top, (8, block))

    old = None if own else carry_ref[40:41, cols]
    if not own:
        set_shift(old)
    total = weigh()
    sums = total[size : size + 1, :]
    fits = jnp.max(sums) < SUM_LIMIT
    if own:
        fits = jnp.logical_and(fits, jnp.min(sums) > 1.0 / SUM_LIMIT)
        finish(total, jnp.zeros((1, block), F32))
    else:
        finish(total + carry_ref[:, cols], old)

    @pl.when(jnp.logical_not(fits))
    def _():
        for j in range(keys // span):
            copy_out(step, j).wait()
        if not own:
            qaug_ref[3 * size : 3 * size + 16, cols] = jnp.where(extra_rows == 0, 1.0, 0.0).astype(
                BF
            )
        top = set_maximum(old)
        again = weigh()
        if not own:
            again = again + jnp.exp2(old - top) * carry_ref[:, cols]
        finish(again, top)

    @pl.when(step == pl.num_programs(0) - 1)
    def _():
        for at in range(kept_ref.shape[0]):
            for j in range(keys // span):
                copy_out(at, j).wait()


def forward_step(lane, beta, queries, kv, carry, last):
    sources, size, part = queries.shape
    count = sources * part
    block = count // 2
    own = carry is None
    vmem = pl.BlockSpec(memory_space=pltpu.VMEM)
    out_shape = (
        jax.ShapeDtypeStruct((count, count), BF),
        jax.ShapeDtypeStruct((48, count), F32),
    )
    if last:
        out_shape = out_shape[:1] + (jax.ShapeDtypeStruct((8, size, count // 8), BF),) + out_shape[1:]
    args = (lane.reshape(1), beta, queries, kv) + (() if own else (carry,))
    return pl.pallas_call(
        partial(forward_kernel, own=own, last=last, size=size, span=count // 8),
        grid=(count // block,),
        in_specs=[pl.BlockSpec(memory_space=pltpu.SMEM)] * 2 + [vmem] * (len(args) - 2),
        out_specs=(pl.BlockSpec(memory_space=pl.ANY),) + tuple(vmem for _ in out_shape[1:]),
        out_shape=out_shape,
        scratch_shapes=[
            pltpu.VMEM((4 * size, count), BF),
            pltpu.VMEM((count, 4 * size), BF),
            pltpu.VMEM((size + 16, count), BF),
            pltpu.VMEM((count // block, count, block), BF),
            pltpu.SemaphoreType.DMA((count // block, 8)),
        ],
        compiler_params=params(1),
        cost_estimate=pl.CostEstimate(
            flops=4 * count * count * 128, bytes_accessed=2**21, transcendentals=count * count
        ),
        name="sample_forward",
    )(*args)


def backward_kernel(
    lane_ref, q_ref, stat_ref, top_ref, do_ref, kv_ref, kept_ref, *rest, first, size, span, piece
):
    if first:
        held_ref = None
    else:
        held_ref, rest = rest[0], rest[1:]
    dq_ref, dkv_ref, factor_ref, daug_ref, vaug_ref, pside_ref, dside_ref, kt_ref = rest
    step = pl.program_id(0)
    block, count = kept_ref.shape

    @pl.when(step == 0)
    def _():
        keys = lay_rows(kv_ref, 0, size).astype(F32)
        kt_ref[...] = jnp.where(keys[0:1, :] > 0.5 * FLAG, 0.0, keys).astype(BF)
        row = lax.broadcasted_iota(jnp.int32, (size, count), 0)
        ones = jnp.where(row < 3, 1.0, 0.0).astype(BF)
        vaug_ref[...] = jnp.concatenate([lay_rows(kv_ref, size, 2 * size), ones], axis=0).T
        lanes = q_ref.shape[0]
        parts = do_ref.shape[0] // lanes
        grads = jnp.concatenate(
            [
                do_ref[(lane ^ lane_ref[0]) * parts + part]
                for lane in range(lanes)
                for part in range(parts)
            ],
            axis=1,
        ).astype(F32)
        delta = -jnp.sum(grads * stat_ref[0:size, :], axis=0, keepdims=True)
        extra = jnp.zeros((size, count), F32)
        for at, part in enumerate(three_parts(delta)):
            extra = jnp.where(row == at, part.astype(F32), extra)
        daug_ref[0:size, :] = grads.astype(BF)
        daug_ref[size : 2 * size, :] = extra.astype(BF)
        factor = jnp.exp2(top_ref[40:41, :] - stat_ref[size : size + 1, :])
        factor_ref[...] = jnp.broadcast_to(factor, factor_ref.shape)
        queries = lay_rows(q_ref, 0, size).astype(F32)
        pside_ref[...] = (grads * factor).astype(BF)
        dside_ref[...] = (queries * factor).astype(BF)
        dq_ref[...] = jnp.zeros(dq_ref.shape, F32)

    sums = [None] * (count // span)
    for i in range(block // piece):
        start = pl.multiple_of(step * block + i * piece, piece)
        rows = pl.ds(start, piece)
        dkeys = None
        for j in range(count // span):
            cols = slice(j * span, (j + 1) * span)
            prob = kept_ref[i * piece : (i + 1) * piece, cols]
            change = dot(vaug_ref[rows, :], daug_ref[:, cols])
            change = (prob.astype(F32) * change).astype(BF)
            terms = (
                dot_last(pside_ref[:, cols], prob),
                dot_last(dside_ref[:, cols], change),
            )
            dkeys = terms if dkeys is None else tuple(x + y for x, y in zip(dkeys, terms))
            term = dot(kt_ref[:, rows], change)
            sums[j] = term if sums[j] is None else sums[j] + term
        dkv_ref[0:size, rows] = dkeys[0].astype(dkv_ref.dtype)
        dkv_ref[size : 2 * size, rows] = dkeys[1].astype(dkv_ref.dtype)
    for j, term in enumerate(sums):
        dq_ref[:, j * span : (j + 1) * span] += term

    @pl.when(step == pl.num_programs(0) - 1)
    def _():
        total = dq_ref[...] * factor_ref[0:1, :]
        dq_ref[...] = total if first else total + held_ref[...]


def backward_step(lane, queries, stat, top, grads, kv, kept, held, kind):
    sources, size, part = queries.shape
    count = sources * part
    block = count // 4
    first = held is None
    vmem = pl.BlockSpec(memory_space=pltpu.VMEM)
    args = (lane.reshape(1), queries, stat, top, grads, kv, kept) + (() if first else (held,))
    return pl.pallas_call(
        partial(
            backward_kernel, first=first, size=size, span=count // 2, piece=count // 8
        ),
        grid=(count // block,),
        in_specs=[pl.BlockSpec(memory_space=pltpu.SMEM)]
        + [vmem] * 5
        + [pl.BlockSpec((block, count), lambda i: (i, 0))]
        + [vmem] * (len(args) - 7),
        out_specs=(vmem, vmem),
        out_shape=(
            jax.ShapeDtypeStruct((size, count), F32),
            jax.ShapeDtypeStruct((2 * size, count), kind),
        ),
        scratch_shapes=[
            pltpu.VMEM((8, count), F32),
            pltpu.VMEM((2 * size, count), BF),
            pltpu.VMEM((count, 2 * size), BF),
            pltpu.VMEM((size, count), BF),
            pltpu.VMEM((size, count), BF),
            pltpu.VMEM((size, count), BF),
        ],
        compiler_params=params(1),
        cost_estimate=pl.CostEstimate(
            flops=count * count * 128, bytes_accessed=2**20, transcendentals=0
        ),
        name="sample_backward",
    )(*args)


def lane_block(shape, block):
    return lax.broadcasted_iota(jnp.int32, shape, 1) // block


def to_tokens(rows8, turn_ref, base, entry):
    tiles = rows8.shape[1] // 128
    per_tile = 128 // entry
    where = lane_block((tiles, 128), entry)
    for j in range(tiles):
        turn_ref[base + j * GROUP : base + (j + 1) * GROUP, :] = rows8[:, j * 128 : (j + 1) * 128]
    by_row = [turn_ref[pl.ds(base + n, tiles, stride=GROUP), :] for n in range(GROUP)]
    strips = []
    for kk in range(per_tile):
        halves = []
        for quad in range(GROUP // per_tile):
            out = jnp.zeros((tiles, 128), F32)
            for i in range(per_tile):
                part = by_row[quad * per_tile + i]
                shift = ((i - kk) * entry) % 128
                if shift:
                    part = pltpu.roll(part, shift, 1)
                out = jnp.where(where == i, part, out)
            halves.append(out)
        strips.append(jnp.concatenate(halves, axis=1))
    return jnp.concatenate(strips, axis=0)


def from_tokens(block, turn_ref, base, entry):
    per_tile = 128 // entry
    tiles = block.shape[0] // per_tile
    where = lane_block((tiles, 128), entry)
    for n in range(GROUP):
        quad, i = divmod(n, per_tile)
        out = jnp.zeros((tiles, 128), F32)
        for kk in range(per_tile):
            part = block[kk * tiles : (kk + 1) * tiles, quad * 128 : (quad + 1) * 128]
            shift = ((kk - i) * entry) % 128
            if shift:
                part = pltpu.roll(part, shift, 1)
            out = jnp.where(where == kk, part, out)
        turn_ref[pl.ds(base + n, tiles, stride=GROUP), :] = out
    return jnp.concatenate(
        [turn_ref[base + j * GROUP : base + (j + 1) * GROUP, :] for j in range(tiles)], axis=1
    )


def heads_in_order(ret_ref, lanes, parts):
    return jnp.concatenate(
        [ret_ref[lane * parts + part] for part in range(parts) for lane in range(lanes)], axis=0
    )


def join_halves(mine_ref, theirs_ref, is_low):
    mine = mine_ref[...].astype(F32)
    theirs = theirs_ref[...].astype(F32)
    return jnp.concatenate(
        [jnp.where(is_low, mine, theirs), jnp.where(is_low, theirs, mine)], axis=1
    )


def turn_kernel_of(part_ref, cmine_ref, ctheirs_ref, c2_ref, turn_ref, *, entry):
    step_rows = cmine_ref.shape[0]
    upstream = join_halves(cmine_ref, ctheirs_ref, part_ref[0] == 0)
    tokens = upstream.shape[1] // entry
    area = upstream.shape[1] // 128 * GROUP
    for g in range(step_rows // GROUP):
        c2_ref[g * tokens : (g + 1) * tokens, :] = to_tokens(
            upstream[g * GROUP : (g + 1) * GROUP], turn_ref, g * area, entry
        ).astype(BF)


def enter_kernel(
    part_ref, x_ref, ret_ref, wout_ref, gain_ref, bias_ref,
    normed_ref, inverse_ref, t2_ref, rows_ref, turn_ref, *, lanes, parts, entry
):
    step = pl.program_id(0)
    step_rows, width = x_ref.shape
    area = width // 128 * GROUP
    tokens = width // entry

    @pl.when(step == 0)
    def _():
        rows_ref[...] = heads_in_order(ret_ref, lanes, parts).astype(F32).T.astype(BF)

    rows = pl.ds(pl.multiple_of(step * step_rows, step_rows), step_rows)
    hidden = x_ref[...].astype(F32) + dot(rows_ref[rows, :], wout_ref[...])
    centred = hidden - jnp.mean(hidden, axis=-1, keepdims=True)
    inverse = lax.rsqrt(jnp.mean(centred * centred, axis=-1, keepdims=True) + NORM_EPS)
    normed = centred * inverse
    normed_ref[...] = normed.astype(BF)
    inverse_ref[...] = jnp.broadcast_to(inverse, inverse_ref.shape)
    unit = normed * gain_ref[...] + bias_ref[...]
    for g in range(step_rows // GROUP):
        t2_ref[g * tokens : (g + 1) * tokens, :] = to_tokens(
            unit[g * GROUP : (g + 1) * GROUP], turn_ref, g * area, entry
        ).astype(BF)


def attend_kernel(
    beta_ref, t2_ref, c2_ref, pres_ref, wq_ref, wk_ref, wv_ref, wot_ref,
    back_ref, grad_ref, maps_ref,
    bm_ref, bn_ref, bm2_ref, bn2_ref, t2t_ref, c2t_ref, qn_ref, xn_ref, xq_ref, place_ref,
    tb_ref, sd_ref, pd_ref, zs_ref, un_ref, wn_ref, *, heads, size
):
    step = pl.program_id(0)
    _, tokens, _ = pres_ref.shape
    step_lanes, packed = t2_ref.shape
    entry = packed // GROUP
    assoc = heads * size
    lanes_all = heads * tokens
    tall = GROUP * tokens
    half_rows = tall // 2
    half_packed = packed // 2
    per_tile = 128 // entry
    part_lanes = 256

    @pl.when(step == 0)
    def _():
        owner = lax.broadcasted_iota(jnp.int32, (assoc, assoc), 0) // entry
        keep = lane_block((assoc, assoc), size) == owner

        def spread(weight_ref):
            tall_weight = jnp.concatenate([weight_ref[...].astype(F32)] * heads, axis=0)
            return jnp.where(keep, tall_weight, 0.0).astype(BF)

        score_map = dot_last(spread(wk_ref), jnp.concatenate([wq_ref[...]] * GROUP, axis=0))
        value_map = dot_last(spread(wv_ref), jnp.concatenate([wot_ref[...]] * GROUP, axis=0))
        place = lane_block((entry, packed), entry)
        for head in range(heads):
            score_rows = score_map[head * entry : (head + 1) * entry] * beta_ref[head]
            value_rows = value_map[head * entry : (head + 1) * entry]
            for n in range(GROUP):
                at = head * packed + n * entry
                bm2_ref[at : at + entry, :] = jnp.where(place == n, score_rows, 0.0).astype(BF)
                bn2_ref[at : at + entry, :] = jnp.where(place == n, value_rows, 0.0).astype(BF)
            span = slice(head * packed, (head + 1) * packed)
            bm_ref[:, span] = bm2_ref[span, :].astype(F32).T.astype(BF)
            bn_ref[:, span] = bn2_ref[span, :].astype(F32).T.astype(BF)
        row_place = lax.broadcasted_iota(jnp.int32, place_ref.shape, 0) // tokens
        place_ref[...] = jnp.where(
            row_place == lane_block(place_ref.shape, entry), 1.0, 0.0
        ).astype(BF)

    all_rows = pl.ds(pl.multiple_of(step * step_lanes, step_lanes), step_lanes)
    t2 = t2_ref[...]
    c2 = c2_ref[...]
    t2t_ref[:, all_rows] = t2.astype(F32).T.astype(BF)
    c2t_ref[:, all_rows] = c2.astype(F32).T.astype(BF)
    qn_ref[...] = dot(t2, bm_ref[...]).astype(BF)
    xn_ref[...] = dot(c2, bn_ref[...]).astype(BF)

    pair_lane = lax.broadcasted_iota(jnp.int32, (tokens, 128), 1) % tokens
    pair_row = lax.broadcasted_iota(jnp.int32, (tokens, 128), 0)
    diagonal = jnp.where(pair_lane == pair_row, 0.0, NEG)
    packed_place = lane_block((tokens, packed), entry)

    groups = step_lanes // tokens

    def score(g):
        own_rows = slice(g * tokens, (g + 1) * tokens)
        base = g * 2 * lanes_all
        for head in range(heads):
            cols = slice(head * packed, (head + 1) * packed)
            at = base + head * tokens
            xq_ref[at : at + tokens, :] = xn_ref[own_rows, cols]
            xq_ref[at + lanes_all : at + lanes_all + tokens, :] = qn_ref[own_rows, cols]
        tb = jnp.concatenate([t2[own_rows]] * GROUP, axis=0) * place_ref[...]
        rows = slice(g * tall, (g + 1) * tall)
        tb_ref[rows, :] = tb
        sd_ref[rows, :] = dot_last(tb, xq_ref[base : base + 2 * lanes_all, :])

    def soften(g):
        present = pres_ref[g]
        for n in range(GROUP):
            at = g * tall + n * tokens
            rows = slice(at, at + tokens)
            mask = jnp.maximum(diagonal, present[:, n : n + 1])
            mask = jnp.concatenate([mask] * (part_lanes // 128), axis=1)
            for part in range(lanes_all // part_lanes):
                span = slice(part * part_lanes, (part + 1) * part_lanes)
                far = slice(lanes_all + part * part_lanes, lanes_all + (part + 1) * part_lanes)
                own_scores = sd_ref[rows, far] + mask
                own_dprob = sd_ref[rows, span]
                terms = jnp.exp(own_scores - jnp.max(own_scores, axis=0, keepdims=True))
                prob = terms * (1.0 / jnp.sum(terms, axis=0, keepdims=True))
                delta = jnp.sum(prob * own_dprob, axis=0, keepdims=True)
                pd_ref[rows, span] = prob.astype(BF)
                pd_ref[rows, far] = (prob * (own_dprob - delta)).astype(BF)

    def gather(g):
        base = g * 2 * lanes_all
        at = g * tall
        tb_first = tb_ref[at : at + half_rows, 0:half_packed].astype(F32).T.astype(BF)
        tb_second = tb_ref[at + half_rows : at + tall, half_packed:].astype(F32).T.astype(BF)
        first_half = dot(tb_first, pd_ref[at : at + half_rows, :]).T.astype(BF)
        second_half = dot(tb_second, pd_ref[at + half_rows : at + tall, :]).T.astype(BF)
        group_rows = pl.ds(pl.multiple_of(step * step_lanes + g * tokens, tokens), tokens)
        for offset, target in ((0, un_ref), (lanes_all, wn_ref)):
            for head in range(heads):
                rows = slice(offset + head * tokens, offset + (head + 1) * tokens)
                cols = head * packed
                target[group_rows, cols : cols + half_packed] = first_half[rows]
                target[group_rows, cols + half_packed : cols + packed] = second_half[rows]
        side = xq_ref[base : base + 2 * lanes_all, :]
        halves = [
            dot(pd_ref[at : at + half_rows, :], side),
            dot(pd_ref[at + half_rows : at + tall, :], side),
        ]
        folded = jnp.zeros((tokens, packed), F32)
        for n in range(GROUP):
            half, row = divmod(n * tokens, half_rows)
            folded = jnp.where(packed_place == n, halves[half][row : row + tokens], folded)
        zs_ref[group_rows, :] = folded

    score(0)
    score(1)
    soften(0)
    for g in range(groups):
        if g + 2 < groups:
            score(g + 2)
        if g + 1 < groups:
            soften(g + 1)
        gather(g)

    @pl.when(step == pl.num_programs(0) - 1)
    def _():
        count = un_ref.shape[0] // 8
        for first in range(0, un_ref.shape[0], count):
            rows = slice(first, first + count)
            back_ref[rows, :] = dot(un_ref[rows, :], bn2_ref[...]).astype(BF)
            grad_ref[rows, :] = (zs_ref[rows, :] + dot(wn_ref[rows, :], bm2_ref[...])).astype(BF)
        value_sums = dot(c2t_ref[...], un_ref[...])
        score_sums = dot(t2t_ref[...], wn_ref[...])
        place = lane_block((entry, packed), entry)
        for d in range(heads):
            folded = []
            for acc in (value_sums, score_sums):
                total = jnp.zeros((entry, packed), F32)
                for n in range(GROUP):
                    piece = acc[n * entry : (n + 1) * entry, d * packed : (d + 1) * packed]
                    total = jnp.where(place == n, piece, total)
                total = total[:, 0:128] + total[:, 128:256]
                total = total + pltpu.roll(total, 64, 1)
                folded.append(total + pltpu.roll(total, 32, 1))
            where = lane_block((entry, 128), entry) == d % per_tile
            both = jnp.concatenate([jnp.where(where, total, 0.0) for total in folded], axis=1)
            maps_ref[d] = both.astype(BF)


def leave_kernel(
    part_ref, normed_ref, inverse_ref, gain_ref, bias_ref, cmine_ref, ctheirs_ref,
    back_ref, grad_ref, wout_ref,
    omine_ref, otheirs_ref, dh_ref, dret_ref, gain_acc, bias_acc, turn_ref,
    *, lanes, parts, entry
):
    step = pl.program_id(0)
    step_rows, width = normed_ref.shape
    area = width // 128 * GROUP
    tokens = width // entry
    half_width = width // parts

    @pl.when(step == 0)
    def _():
        gain_acc[...] = jnp.zeros(gain_acc.shape, F32)
        bias_acc[...] = jnp.zeros(bias_acc.shape, F32)

    is_low = part_ref[0] == 0
    changes = []
    token_grads = []
    for g in range(step_rows // GROUP):
        span = slice(g * tokens, (g + 1) * tokens)
        changes.append(from_tokens(back_ref[span, :].astype(F32), turn_ref, (2 * g) * area, entry))
        token_grads.append(from_tokens(grad_ref[span, :].astype(F32), turn_ref, (2 * g + 1) * area, entry))
    normed = normed_ref[...].astype(F32)
    gain = gain_ref[...]
    unit = normed * gain + bias_ref[...]
    out = (unit + jnp.concatenate(changes, axis=0)).astype(BF)
    low_out, high_out = out[:, :half_width], out[:, half_width:]
    omine_ref[...] = jnp.where(is_low, low_out, high_out)
    otheirs_ref[...] = jnp.where(is_low, high_out, low_out)
    dunit = join_halves(cmine_ref, ctheirs_ref, is_low) + jnp.concatenate(token_grads, axis=0)
    gain_acc[...] += jnp.sum(dunit * normed, axis=0, keepdims=True)
    bias_acc[...] += jnp.sum(dunit, axis=0, keepdims=True)
    dn = dunit * gain
    dhidden = inverse_ref[:, 0:1] * (
        dn
        - jnp.mean(dn, axis=-1, keepdims=True)
        - normed * jnp.mean(dn * normed, axis=-1, keepdims=True)
    )
    dh_ref[pl.ds(pl.multiple_of(step * step_rows, step_rows), step_rows), :] = dhidden.astype(BF)

    @pl.when(step == pl.num_programs(0) - 1)
    def _():
        size = dret_ref.shape[1]
        dret = dot_last(wout_ref[...], dh_ref[...]).astype(BF)
        for part in range(parts):
            for lane in range(lanes):
                head = part * lanes + lane
                dret_ref[lane * parts + part] = dret[head * size : (head + 1) * size]


def pack_kernel(ret_ref, dh_ref, gain_ref, bias_ref, maps_ref, pack_ref, *, lanes, parts):
    dests, _, cols = pack_ref.shape
    turned = heads_in_order(ret_ref, lanes, parts)
    assoc = turned.shape[0]
    out_grad = dot(turned, dh_ref[...]).astype(BF)
    row = lax.broadcasted_iota(jnp.int32, (16, cols), 0)
    for d in range(dests):
        span = slice(d * cols, (d + 1) * cols)
        pack_ref[d, 0:assoc, :] = out_grad[:, span]
        sums = jnp.where(row == 0, gain_ref[:, span], jnp.where(row == 1, bias_ref[:, span], 0.0))
        pack_ref[d, assoc : assoc + 16, :] = sums.astype(BF)
        pack_ref[d, assoc + 16 :, :] = maps_ref[d]


def make_pack(ret, dhidden, gain_sum, bias_sum, maps, parts):
    heads, size, _ = ret.shape
    entry = maps.shape[1]
    width = dhidden.shape[1]
    vmem = pl.BlockSpec(memory_space=pltpu.VMEM)
    return pl.pallas_call(
        partial(pack_kernel, lanes=heads // parts, parts=parts),
        in_specs=[vmem] * 5,
        out_specs=vmem,
        out_shape=jax.ShapeDtypeStruct((heads, heads * size + 16 + entry, width // heads), BF),
        compiler_params=params(),
        cost_estimate=pl.CostEstimate(flops=2**28, bytes_accessed=2**22, transcendentals=0),
        name="pack",
    )(ret, dhidden, gain_sum, bias_sum, maps)


def turn_cotangent(part, cot_mine, cot_theirs, parts, entry):
    half, half_width = cot_theirs.shape
    width = half_width * parts
    step_rows = GROUP * EDGE_GROUPS
    steps = half // step_rows
    step_lanes = EDGE_GROUPS * (width // entry)
    return pl.pallas_call(
        partial(turn_kernel_of, entry=entry),
        grid_spec=pltpu.PrefetchScalarGridSpec(
            num_scalar_prefetch=1,
            grid=(steps,),
            in_specs=[
                pl.BlockSpec((step_rows, half_width), lambda i, part: (part[0] * steps + i, 0)),
                pl.BlockSpec((step_rows, half_width), lambda i, part: (i, 0)),
            ],
            out_specs=pl.BlockSpec((step_lanes, GROUP * entry), lambda i, part: (i, 0)),
            scratch_shapes=[pltpu.VMEM((EDGE_GROUPS * (width // 128) * GROUP, 128), F32)],
        ),
        out_shape=jax.ShapeDtypeStruct((half // GROUP * (width // entry), GROUP * entry), BF),
        compiler_params=params(1),
        cost_estimate=pl.CostEstimate(flops=2**24, bytes_accessed=2**22, transcendentals=0),
        name="turn_cotangent",
    )(part.reshape(1), cot_mine, cot_theirs)


def middle(
    part_index, inputs, ret, w_out, gain, bias, cot_mine, cot_theirs, c2, present, feats, parts
):
    wq, wk, wv, wo, beta = feats
    rows, width = inputs.shape
    half = rows // parts
    heads, size, _ = ret.shape
    lanes = heads // parts
    tokens = present.shape[1]
    entry = width // tokens
    packed = GROUP * entry
    assoc = heads * size
    steps = half // (GROUP * STEP_GROUPS)
    edge_rows = GROUP * EDGE_GROUPS
    edge_steps = half // edge_rows
    edge_lanes = EDGE_GROUPS * tokens
    half_width = width // parts
    lanes_all = heads * tokens
    step_lanes = STEP_GROUPS * tokens
    all_lanes = half // GROUP * tokens
    vmem = pl.BlockSpec(memory_space=pltpu.VMEM)
    smem = pl.BlockSpec(memory_space=pltpu.SMEM)

    def own(shape):
        return pl.BlockSpec(shape, lambda i, part: (part[0] * edge_steps + i, 0))

    def stepped(shape):
        return pl.BlockSpec(shape, lambda i, *_: (i,) + (0,) * (len(shape) - 1))

    def array(shape, kind):
        return jax.ShapeDtypeStruct(shape, kind)

    part = part_index.reshape(1)
    gain = gain.reshape(1, width)
    bias = bias.reshape(1, width)
    turn = pltpu.VMEM((2 * EDGE_GROUPS * (width // 128) * GROUP, 128), F32)
    normed, inverse, t2 = pl.pallas_call(
        partial(enter_kernel, lanes=lanes, parts=parts, entry=entry),
        grid_spec=pltpu.PrefetchScalarGridSpec(
            num_scalar_prefetch=1,
            grid=(edge_steps,),
            in_specs=[own((edge_rows, width)), vmem, vmem, vmem, vmem],
            out_specs=[
                stepped((edge_rows, width)),
                stepped((edge_rows, 128)),
                stepped((edge_lanes, packed)),
            ],
            scratch_shapes=[pltpu.VMEM((half, assoc), BF), turn],
        ),
        out_shape=(
            array((half, width), BF),
            array((half, 128), F32),
            array((all_lanes, packed), BF),
        ),
        compiler_params=params(1),
        cost_estimate=pl.CostEstimate(flops=2**28, bytes_accessed=2**23, transcendentals=0),
        name="enter",
    )(part, inputs, ret, w_out, gain, bias)

    natural = pltpu.VMEM((all_lanes, heads * packed), BF)
    back, grad, maps = pl.pallas_call(
        partial(attend_kernel, heads=heads, size=size),
        grid=(steps,),
        in_specs=[
            smem,
            stepped((step_lanes, packed)),
            stepped((step_lanes, packed)),
            stepped((STEP_GROUPS, tokens, GROUP)),
            vmem,
            vmem,
            vmem,
            vmem,
        ],
        out_specs=[vmem, vmem, vmem],
        out_shape=(
            array((all_lanes, packed), BF),
            array((all_lanes, packed), BF),
            array((heads, entry, packed), BF),
        ),
        scratch_shapes=[
            pltpu.VMEM((packed, heads * packed), BF),
            pltpu.VMEM((packed, heads * packed), BF),
            pltpu.VMEM((heads * packed, packed), BF),
            pltpu.VMEM((heads * packed, packed), BF),
            pltpu.VMEM((packed, all_lanes), BF),
            pltpu.VMEM((packed, all_lanes), BF),
            pltpu.VMEM((step_lanes, heads * packed), BF),
            pltpu.VMEM((step_lanes, heads * packed), BF),
            pltpu.VMEM((STEP_GROUPS * 2 * lanes_all, packed), BF),
            pltpu.VMEM((GROUP * tokens, packed), BF),
            pltpu.VMEM((STEP_GROUPS * GROUP * tokens, packed), BF),
            pltpu.VMEM((STEP_GROUPS * GROUP * tokens, 2 * lanes_all), F32),
            pltpu.VMEM((STEP_GROUPS * GROUP * tokens, 2 * lanes_all), BF),
            pltpu.VMEM((all_lanes, packed), F32),
            natural,
            natural,
        ],
        compiler_params=params(1),
        cost_estimate=pl.CostEstimate(
            flops=2 * 1200 * half * 256 * 256,
            bytes_accessed=2**23,
            transcendentals=half * heads * tokens * tokens,
        ),
        name="attend",
    )(beta, t2, c2, present, wq, wk, wv, wo)

    out_mine, out_theirs, dhidden, dret, gain_sum, bias_sum = pl.pallas_call(
        partial(leave_kernel, lanes=lanes, parts=parts, entry=entry),
        grid_spec=pltpu.PrefetchScalarGridSpec(
            num_scalar_prefetch=1,
            grid=(edge_steps,),
            in_specs=[
                stepped((edge_rows, width)),
                stepped((edge_rows, 128)),
                vmem,
                vmem,
                own((edge_rows, half_width)),
                stepped((edge_rows, half_width)),
                stepped((edge_lanes, packed)),
                stepped((edge_lanes, packed)),
                vmem,
            ],
            out_specs=[
                stepped((edge_rows, half_width)),
                stepped((edge_rows, half_width)),
                vmem,
                vmem,
                vmem,
                vmem,
            ],
            scratch_shapes=[turn],
        ),
        out_shape=(
            array((half, half_width), BF),
            array((half, half_width), BF),
            array((half, width), BF),
            array((heads, size, half), BF),
            array((1, width), F32),
            array((1, width), F32),
        ),
        compiler_params=params(1),
        cost_estimate=pl.CostEstimate(flops=2**28, bytes_accessed=2**23, transcendentals=0),
        name="leave",
    )(part, normed, inverse, gain, bias, cot_mine, cot_theirs, back, grad, w_out)
    return out_mine, out_theirs, dhidden, dret, gain_sum, bias_sum, maps


def weight_grad_kernel(
    place_ref, beta_ref, dq_ref, term_ref, moved_ref, x_ref, rows_ref, *rest, size
):
    outs, (whole_ref, joined_ref, held_ref, sem) = rest[:-4], rest[-4:]
    blocks, _, width = held_ref.shape
    copies = [
        pltpu.make_async_copy(
            x_ref.at[:, at * width : (at + 1) * width], held_ref.at[at], sem.at[at]
        )
        for at in range(blocks)
    ]
    for copy in copies:
        copy.start()
    rows = rows_ref.shape[2]
    lanes = joined_ref.shape[1] // rows
    parts = rows_ref.shape[0] // lanes
    beta = beta_ref[0]
    dkv = term_ref[...] + moved_ref[...].astype(F32)
    joined = jnp.concatenate([dq_ref[...] * beta, dkv[size:] * beta, dkv[:size]], axis=0)
    joined = joined.astype(BF)
    for relative in range(lanes):
        block = joined[:, relative * rows : (relative + 1) * rows]
        other = relative ^ place_ref[0]
        joined_ref[:, pl.ds(pl.multiple_of(other * rows, rows), rows)] = block
        for part in range(parts):
            rows_ref[other * parts + part] = block
    for at in range(blocks):
        copies[at].wait()
        whole_ref[:, at * width : (at + 1) * width] = dot(joined_ref[...], held_ref[at]).astype(BF)
    slabs, _, piece = outs[0].shape if len(outs) == 1 else (len(outs),) + outs[0].shape
    for r in range(slabs):
        if len(outs) == 1:
            outs[0][r ^ place_ref[2]] = whole_ref[:, r * piece : (r + 1) * piece]
        else:
            start = pl.multiple_of((r ^ place_ref[2]) * piece, piece)
            outs[r][...] = whole_ref[:, pl.ds(start, piece)]


def weight_grads(place, beta, dq, term, moved, slab_inputs, lanes, slabs, parts):
    size = dq.shape[0]
    three = 3 * size
    total, width = slab_inputs.shape
    rows = total // lanes
    piece = width // slabs
    vmem = pl.BlockSpec(memory_space=pltpu.VMEM)
    smem = pl.BlockSpec(memory_space=pltpu.SMEM)
    if piece % 128:
        shapes = [jax.ShapeDtypeStruct((slabs, three, piece), BF)]
    else:
        shapes = [jax.ShapeDtypeStruct((three, piece), BF)] * slabs
    dqkv_rows, *grads = pl.pallas_call(
        partial(weight_grad_kernel, size=size),
        in_specs=[smem, smem, vmem, vmem, vmem, pl.BlockSpec(memory_space=pl.ANY)],
        out_specs=[vmem] * (1 + len(shapes)),
        out_shape=[jax.ShapeDtypeStruct((lanes * parts, three, rows), BF)] + shapes,
        scratch_shapes=[
            pltpu.VMEM((three, width), BF),
            pltpu.VMEM((three, total), BF),
            pltpu.VMEM((4, total, width // 4), BF),
            pltpu.SemaphoreType.DMA((4,)),
        ],
        compiler_params=params(),
        cost_estimate=pl.CostEstimate(flops=2**20, bytes_accessed=2**16, transcendentals=0),
        name="weight_grads",
    )(place, beta, dq, term, moved, slab_inputs)
    return dqkv_rows, grads[0] if piece % 128 else grads


def input_grad_kernel(
    place_ref, x_ref, *rest, lanes, size
):
    wm_ref, wt_ref, dm_ref, du_ref, dl_ref, out_ref, mine_ref, theirs_ref = rest
    part = place_ref[1]
    parts = x_ref.shape[0] // lanes

    @pl.when(pl.program_id(0) == 0)
    def _():
        for source, target in ((part, mine_ref), (parts - 1 - part, theirs_ref)):
            blocks = [
                x_ref[lane * parts + source, kind * size : (kind + 1) * size, :]
                for kind in range(3)
                for lane in range(lanes)
            ]
            target[...] = jnp.concatenate(blocks, axis=0).T

    wm = jnp.concatenate([wm_ref[kind] for kind in range(3)], axis=1)
    wt = jnp.concatenate([wt_ref[kind] for kind in range(3)], axis=1)
    out = dot_last(mine_ref[...], wm) + dot_last(theirs_ref[...], wt)
    half = dm_ref.shape[0]
    mine = dm_ref[...].astype(F32)
    theirs = jnp.concatenate([du_ref[...], dl_ref[...]], axis=0).astype(F32)
    is_low = part == 0
    out_ref[0:half, :] = (out[0:half] + jnp.where(is_low, mine, theirs)).astype(BF)
    out_ref[half:, :] = (out[half:] + jnp.where(is_low, theirs, mine)).astype(BF)


def input_grads(place, dqkv_rows, w_mine, w_theirs, dh_mine, dh_upper, dh_lower, lanes):
    _, three, rows = dqkv_rows.shape
    _, width, local = w_mine.shape
    half = dh_mine.shape[0]
    block = width // 2
    weight = pl.BlockSpec((3, block, local), lambda i: (0, i, 0))
    residual = pl.BlockSpec((half, block), lambda i: (0, i))
    return pl.pallas_call(
        partial(input_grad_kernel, lanes=lanes, size=three // 3),
        grid=(width // block,),
        in_specs=[
            pl.BlockSpec(memory_space=pltpu.SMEM),
            pl.BlockSpec(memory_space=pltpu.VMEM),
        ]
        + [weight] * 2
        + [residual]
        + [pl.BlockSpec((half // 2, block), lambda i: (0, i))] * 2,
        out_specs=pl.BlockSpec((rows, block), lambda i: (0, i)),
        out_shape=jax.ShapeDtypeStruct((rows, width), BF),
        scratch_shapes=[pltpu.VMEM((rows, 3 * local), BF)] * 2,
        compiler_params=params(1),
        cost_estimate=pl.CostEstimate(flops=2**20, bytes_accessed=2**16, transcendentals=0),
        name="input_grads",
    )(place, dqkv_rows, w_mine, w_theirs, dh_mine, dh_upper, dh_lower)


def turn_kernel(place_ref, beta_ref, *rest, size):
    kinds, rest = rest[:4], rest[4:]
    wq_ref, gq_ref, gk_ref, gv_ref, sum_ref, acc_ref, hold_ref = rest
    step = pl.program_id(0)
    for kind, kind_ref in enumerate(kinds):
        hold_ref[kind] = kind_ref[0]

    side, odd = place_ref[0] // 2, place_ref[0] % 2
    pieces = [
        hold_ref[2 * ((lane % 2) ^ odd) + ((lane // 2) ^ side)].astype(F32) for lane in range(4)
    ]
    for place, target in enumerate((gq_ref, gk_ref, gv_ref)):
        target[...] = jnp.concatenate(
            [piece[place * size : (place + 1) * size] for piece in pieces], axis=0
        ).T
    product = jnp.sum(gq_ref[...] * wq_ref[...].astype(F32), axis=0, keepdims=True)

    @pl.when(step == 0)
    def _():
        acc_ref[...] = product

    @pl.when(step > 0)
    def _():
        acc_ref[...] += product

    @pl.when(step == pl.num_programs(0) - 1)
    def _():
        total = acc_ref[...]
        owner = lane_block(total.shape, size)
        at = lax.broadcasted_iota(jnp.int32, (1, 128), 1)
        sums = jnp.zeros((1, 128), F32)
        for lane in range(len(pieces)):
            own = jnp.sum(jnp.where(owner == lane, total, 0.0), axis=1, keepdims=True)
            sums = jnp.where(at == lane, own / beta_ref[lane], sums)
        sum_ref[...] = sums[:, 0 : len(pieces)]


def turn_grads(place, beta, blocks, w_query):
    slabs, three, piece = blocks[0].shape
    lanes = len(blocks)
    size = three // 3
    source = pl.BlockSpec((1, three, piece), lambda i, at: (i ^ at[2], 0, 0))
    target = pl.BlockSpec((piece, lanes * size), lambda i, at: (i, 0))
    shape = jax.ShapeDtypeStruct((slabs * piece, lanes * size), F32)
    return pl.pallas_call(
        partial(turn_kernel, size=size),
        grid_spec=pltpu.PrefetchScalarGridSpec(
            num_scalar_prefetch=1,
            grid=(slabs,),
            in_specs=[pl.BlockSpec(memory_space=pltpu.SMEM)] + [source] * lanes + [target],
            out_specs=[target, target, target, pl.BlockSpec((1, lanes), lambda i, at: (0, 0))],
            scratch_shapes=[
                pltpu.VMEM((1, lanes * size), F32),
                pltpu.VMEM((lanes, three, piece), BF),
            ],
        ),
        out_shape=(shape, shape, shape, jax.ShapeDtypeStruct((1, lanes), F32)),
        compiler_params=params(1),
        cost_estimate=pl.CostEstimate(flops=0, bytes_accessed=2**16, transcendentals=0),
        name="turn_grads",
    )(place, beta, *blocks, w_query)


def unpack_kernel(
    place_ref, beta_ref, near_ref, far_ref, wq_ref, wk_ref, wv_ref, wo_ref,
    out_ref, gain_ref, bias_ref, fq_ref, fk_ref, fv_ref, fo_ref, fb_ref, *, size
):
    parts, sides, _, cols = near_ref.shape
    heads = 2 * sides * parts
    assoc = heads * size
    entry = wq_ref.shape[0]
    side, even, part = place_ref[0] // 2, place_ref[0] % 2 == 0, place_ref[1]
    per_tile = 128 // entry
    tiles = heads // per_tile
    maps = [[jnp.zeros((entry, 128), F32) for _ in range(tiles)] for _ in range(4)]
    for d in range(heads):
        lane, of_part = divmod(d, parts)
        of_side, odd = divmod(lane, 2)
        at_part = (of_part + part) % parts
        at_side = (of_side + side) % sides
        near = near_ref[at_part, at_side].astype(F32)
        far = far_ref[at_part, at_side].astype(F32)
        whole = jnp.where(even, far if odd else near, near if odd else far)
        span = slice(d * cols, (d + 1) * cols)
        out_ref[:, span] = whole[0:assoc]
        gain_ref[:, span] = whole[assoc : assoc + 1]
        bias_ref[:, span] = whole[assoc + 1 : assoc + 2]
        block = whole[assoc + 16 : assoc + 16 + entry]
        tile, slot = divmod(d, per_tile)
        for kind in range(2):
            piece = block[:, kind * 128 : (kind + 1) * 128]
            square = jnp.concatenate([piece, jnp.zeros((128 - entry, 128), F32)], axis=0).T
            turned = square[slot * entry : (slot + 1) * entry]
            if slot:
                turned = pltpu.roll(turned, slot * entry, 1)
            maps[2 * kind][tile] = maps[2 * kind][tile] + piece
            maps[2 * kind + 1][tile] = maps[2 * kind + 1][tile] + turned
    value_turned, value, score_turned, score = [
        jnp.concatenate(tile_list, axis=1).astype(BF) for tile_list in maps
    ]
    lane = lax.broadcasted_iota(jnp.int32, (assoc, assoc), 1) // size
    owner = lax.broadcasted_iota(jnp.int32, (assoc, assoc), 0) // entry

    def spread(weights):
        tall = jnp.concatenate([weights.astype(F32)] * heads, axis=0)
        return jnp.where(lane == owner, tall, 0.0).astype(BF)

    scale = jnp.zeros((1, assoc), F32)
    for head in range(heads):
        scale = jnp.where(lane[0:1] == head, beta_ref[head], scale)
    fq = dot(score_turned, spread(wk_ref[...]))
    fq_ref[...] = fq * scale
    fk_ref[...] = dot(score, spread(wq_ref[...])) * scale
    fv_ref[...] = dot(value, spread(wo_ref[...]))
    fo_ref[...] = dot(value_turned, spread(wv_ref[...]))
    sums = jnp.sum(fq * wq_ref[...].astype(F32), axis=0, keepdims=True)
    at = lax.broadcasted_iota(jnp.int32, (1, 128), 1)
    each = jnp.zeros((1, 128), F32)
    for head in range(heads):
        own = jnp.sum(jnp.where(lane[0:1] == head, sums, 0.0), axis=1, keepdims=True)
        each = jnp.where(at == head, own, each)
    fb_ref[...] = each[:, 0:heads]


def unpack(place, beta, near, far, wq, wk, wv, wo, size):
    parts, sides, _, cols = near.shape
    heads = 2 * sides * parts
    width = heads * cols
    vmem = pl.BlockSpec(memory_space=pltpu.VMEM)
    smem = pl.BlockSpec(memory_space=pltpu.SMEM)
    shapes = [(heads * size, width), (1, width), (1, width)]
    shapes += [wq.shape, wk.shape, wv.shape, wo.shape, (1, heads)]
    return pl.pallas_call(
        partial(unpack_kernel, size=size),
        in_specs=[smem, smem] + [vmem] * 6,
        out_specs=tuple(vmem for _ in shapes),
        out_shape=tuple(jax.ShapeDtypeStruct(shape, F32) for shape in shapes),
        compiler_params=params(),
        cost_estimate=pl.CostEstimate(flops=2**20, bytes_accessed=2**16, transcendentals=0),
        name="unpack",
    )(place, beta, near, far, wq, wk, wv, wo)


def tie(*values):
    return lax.optimization_barrier(values)


def body(
    inputs,
    memory_keep,
    feature_present,
    w_query,
    w_key,
    w_value,
    beta_sample,
    w_out,
    norm_gain,
    norm_bias,
    wf_query,
    wf_key,
    wf_value,
    beta_feature,
    wf_out,
    cotangent,
):
    rows, width = inputs.shape
    lanes = beta_sample.shape[0]
    parts = lax.axis_size("heads")
    slabs = lax.axis_size("slab")
    lane = lax.axis_index("lane")
    part = lax.axis_index("heads")
    half = rows // parts
    size = w_query.shape[1] // lanes
    tokens = feature_present.shape[1]
    entry = width // tokens
    heads = lanes * parts
    flip = [(i, (i + 1) % parts) for i in range(parts)]
    ring = [(i, (i + 1) % slabs) for i in range(slabs)]
    group = ("lane", "heads")

    def spread(x, axes):
        return lax.all_to_all(x, axes, split_axis=0, concat_axis=0, tiled=True)

    place = jnp.stack([lane, part, lax.axis_index("slab")]).astype(jnp.int32)

    def swap(x, axes, count, bits):
        return lax.ppermute(x, axes, [(i, i ^ bits) for i in range(count)])

    *pieces, weights_mine = project(
        lane, inputs, w_query, w_key, w_value, memory_keep, lanes
    )
    pieces = [pieces[0]] + [swap(pieces[r], "lane", lanes, r) for r in range(1, lanes)]
    queries = jnp.stack([piece[:size] for piece in pieces])
    beta = lax.dynamic_slice_in_dim(beta_sample, lane, 1, 0)

    held = [jnp.stack([piece[size:] for piece in pieces])]
    kept = []
    tops = []
    carry = None
    for step in range(slabs):
        if step + 1 < slabs:
            held.append(lax.ppermute(held[-1], "slab", ring))
        outs = forward_step(lane, beta, queries, held[step], carry, step + 1 == slabs)
        kept.append(outs[0])
        carry = outs[-1]
        tops.append(carry)
        if step + 1 < slabs:
            held[-1], carry = tie(held[-1], carry)
        if step == 0:
            carry, inputs_late, cot_late = tie(carry, inputs, cotangent)
            slab_inputs = lax.all_gather(inputs_late, "lane", axis=0, tiled=True)
            other_start = (parts - 1 - part) * half
            cot_theirs = lax.ppermute(
                lax.dynamic_slice_in_dim(cot_late, other_start, half, 0), "heads", flip
            )
    _, ret, stat = outs
    ret = spread(ret, group)
    c2 = turn_cotangent(part, cotangent, cot_theirs, parts, entry)
    ret, c2, weights_mine = tie(ret, c2, weights_mine)
    weights_theirs = lax.ppermute(weights_mine, "heads", flip)

    own_present = lax.dynamic_slice_in_dim(feature_present, part * half, half, 0)
    present = own_present.reshape(half // GROUP, GROUP, tokens * entry // 128, 128 // entry)
    present = present.transpose(0, 3, 2, 1).reshape(half // GROUP, tokens, GROUP)
    present = jnp.where(present > 0, 0.0, NEG).astype(F32)
    feats = (wf_query, wf_key, wf_value, wf_out.T, beta_feature)
    out_mine, out_theirs, dhidden, dret, gain_sum, bias_sum, maps = middle(
        part,
        inputs,
        ret,
        w_out,
        norm_gain,
        norm_bias,
        cotangent,
        cot_theirs,
        c2,
        present,
        feats,
        parts,
    )
    dret = spread(dret, group)
    pack = make_pack(ret, dhidden, gain_sum, bias_sum, maps, parts)
    pack, dret, weights_theirs = tie(pack, dret, weights_theirs)
    pack = spread(pack, group)

    dq = None
    moved = None
    bit = 1
    for step in range(slabs):
        at = (step + 1) % slabs
        last = step + 1 == slabs
        dq, term = backward_step(
            lane, queries, stat, tops[at], dret, held[at], kept[at], dq, F32 if last else BF
        )
        if last:
            break
        total = term if moved is None else (term.astype(F32) + moved.astype(F32)).astype(BF)
        total, dq = tie(total, dq)
        moved = lax.ppermute(total, "slab", ring)
        if step == 0:
            upper, dq = tie(dhidden[: half // 2], dq)
            upper = lax.ppermute(upper, "heads", flip)
        elif step == 1:
            upper, lower, dq = tie(upper, dhidden[half // 2 :], dq)
            lower = lax.ppermute(lower, "heads", flip)
        elif step == 2:
            lower, out_theirs, dq = tie(lower, out_theirs, dq)
            out_other = lax.ppermute(out_theirs, "heads", flip)
        if step == 1:
            pack, dq = tie(pack.astype(F32).sum(axis=0).astype(BF), dq)
        elif step > 1 and bit < slabs:
            pack, dq = tie((pack.astype(F32) + pack_other.astype(F32)).astype(BF), dq)
            bit *= 2
        if step > 0 and bit < slabs:
            pack_other = swap(pack, "slab", slabs, bit)
    term, out_other = tie(term, out_other)
    if bit < slabs:
        term, pack_other = tie(term, pack_other)

    dqkv_rows, grads = weight_grads(
        place, beta, dq, term, moved, slab_inputs, lanes, slabs, parts
    )
    if bit < slabs:
        pack, pack_other, dqkv_rows = tie(pack, pack_other, dqkv_rows)
        pack = (pack.astype(F32) + pack_other.astype(F32)).astype(BF)
    terms = [grads[0]] + [swap(grads[r], "slab", slabs, r) for r in range(1, slabs)]
    *terms, dqkv_rows = tie(*terms, dqkv_rows)
    dqkv_rows = spread(dqkv_rows, group)
    grads = sum(term.astype(F32) for term in terms).astype(BF)
    grads = jnp.stack([grads] + [swap(grads, "slab", slabs, r) for r in range(1, slabs)])
    far = swap(grads, "lane", lanes, lanes // 2)
    near = swap(grads, "lane", lanes, 1)
    pack, dqkv_rows = tie(pack, dqkv_rows)
    pack_far = [swap(pack, group, heads, bits) for bits in (1, heads // 2, heads // 2 + 1)]
    input_grad = input_grads(
        place, dqkv_rows, weights_mine, weights_theirs, dhidden, upper, lower, lanes
    )
    *pack_far, input_grad = tie(*pack_far, input_grad)
    pack = jnp.stack([jnp.stack([pack, pack_far[1]]), jnp.stack([pack_far[0], pack_far[2]])])
    pack_near = swap(pack, "lane", lanes, 1)
    sum_out, sum_gain, sum_bias, sum_fquery, sum_fkey, sum_fvalue, sum_fout, fbeta = unpack(
        place, beta_feature, pack, pack_near, wf_query, wf_key, wf_value, wf_out.T, size
    )
    is_low = part == 0
    block_out = jnp.concatenate(
        [jnp.where(is_low, out_mine, out_other), jnp.where(is_low, out_other, out_mine)], axis=0
    )
    far, input_grad, block_out, near = tie(far, input_grad, block_out, near)
    near_far = swap(far, "lane", lanes, 1)
    sum_wquery, sum_wkey, sum_wvalue, sums = turn_grads(
        place, beta_sample, [grads, far, near, near_far], w_query
    )
    return (
        block_out,
        input_grad,
        sum_wquery,
        sum_wkey,
        sum_wvalue,
        sums.reshape(lanes),
        sum_out,
        sum_gain.reshape(width),
        sum_bias.reshape(width),
        sum_fquery,
        sum_fkey,
        sum_fvalue,
        fbeta.reshape(heads),
        sum_fout.T,
    )


def solution(mesh):
    parts = mesh.shape["heads"]
    lanes = 8 // parts
    fine = Mesh(mesh.devices.reshape(-1, lanes, parts), ("slab", "lane", "heads"))
    rows = ("slab", "lane")
    in_specs = (
        P(rows, None),
        P(rows),
        P(rows, None),
        P(None, "heads"),
        P(None, "heads"),
        P(None, "heads"),
        P("heads"),
        P(),
        P(),
        P(),
        P(),
        P(),
        P(),
        P(),
        P(),
        P(rows, "heads"),
    )
    out_specs = (
        P(rows, "heads"),
        P(rows, None),
        P(None, "heads"),
        P(None, "heads"),
        P(None, "heads"),
        P("heads"),
        P(),
        P(),
        P(),
        P(),
        P(),
        P(),
        P(),
        P(),
    )
    return jax.shard_map(body, mesh=fine, in_specs=in_specs, out_specs=out_specs, check_vma=False)
```
